128 devices in a mesh: member: 32 (over z, x, core), section: 4 (over y).
Axes of the slice: x: 4, y: 4, z: 4, core: 2. Of those that a mesh axis runs over, the one named last changes fastest.
Arguments:
- inputs: bfloat16 [32, 2, 1, 14, 14, 512], P('member'), may hold values from -6 to 6
- cotangent: bfloat16 [32, 2, 1, 14, 14, 512], P('member'), may hold values from -6 to 6
- probe: bfloat16 [32, 1, 14, 14, 512], P('member'), may hold values from -6 to 6
- dw_kernel: float32 [32, 4, 7, 7, 512], P('member', 'section'), may hold values from -0.875 to 0.875
- dw_bias: float32 [32, 4, 512], P('member', 'section'), may hold values from -3 to 3
- norm_gain: float32 [32, 4, 512], P('member', 'section'), may hold values from 0.5 to 1.5
- norm_bias: float32 [32, 4, 512], P('member', 'section'), may hold values from -3 to 3
- w_in: float32 [32, 4, 512, 2048], P('member', 'section'), may hold values from -0.25 to 0.25
- b_in: float32 [32, 4, 2048], P('member', 'section'), may hold values from -3 to 3
- w_out: float32 [32, 4, 2048, 512], P('member', 'section'), may hold values from -0.125 to 0.125
- b_out: float32 [32, 4, 512], P('member', 'section'), may hold values from -3 to 3
- layer_scale: float32 [32, 4, 512], P('member', 'section'), may hold values from 0.3 to 1.5
- shuffle_mask: int32 [4, 32], P('section'), may hold values from 0 to 1, as said below
- source_member: int32 [4, 32, 32], P('section'), may hold values from 0 to 31, as said below
Outputs:
- new_w_in: float32 [32, 4, 512, 2048], P('member', 'section')
- new_w_out: float32 [32, 4, 2048, 512], P('member', 'section')
- features: bfloat16 [32, 4, 1, 14, 14, 512], P('member', 'section')
The draws below stay inside these ranges and needn't reach their ends.
Inputs may be any that keep to these rules, and one draw needn't show every extreme that they name: `shuffle_mask`: each section marks exactly 16 of its 32 blocks. Each source_member[s, k] is a permutation of the members. For the marked blocks of a section no member is its own source, and no member is the source of more than 1 of another member's blocks; some pair of members reaches 1 in every section.
All inputs are finite; a program needn't handle non-finite values.
Results may differ from the reference program's by a relative error of at most 0.014.
Values may be sent and summed in bfloat16 or wider, within the bound.
A program may use at most 192 MiB of HBM per device.

```python
import math
import jax
import jax.numpy as jnp
from jax import lax

D = 512
HID = 2048
TILE = 128
SIDE = 14
MICRO = 2
IMGS = 1
MEMBERS = 32
SECTIONS = 4
BLOCKS = 32
SHUFFLED = 16


def shuffle_tables(key):
    masks = []
    tables = []
    for section in range(SECTIONS):
        base = jax.random.fold_in(key, 7919 + section)
        key_blocks, key_shifts, key_labels = jax.random.split(base, 3)
        order_blocks = jax.random.permutation(key_blocks, BLOCKS)
        ranking = jnp.argsort(order_blocks).astype(jnp.int32)
        masks.append((ranking < SHUFFLED).astype(jnp.int32))
        shifts = (jax.random.permutation(key_shifts, MEMBERS - 1) + 1).astype(jnp.int32)
        offsets = shifts[ranking % (MEMBERS - 1)]
        labels = jax.random.permutation(key_labels, MEMBERS).astype(jnp.int32)
        inverse = jnp.argsort(labels).astype(jnp.int32)
        tables.append(inverse[(labels[None, :] - offsets[:, None]) % MEMBERS])
    return (jnp.stack(masks).astype(jnp.int32), jnp.stack(tables).astype(jnp.int32))


def draw_shuffle_mask(key, part):
    return shuffle_tables(jax.random.fold_in(key, 31))[0]


def draw_source_member(key, part):
    return shuffle_tables(jax.random.fold_in(key, 31))[1]


def steps_of(rng, shape, pieces, smallest, top_value):
    level = 1.0
    for axis_at, shards_of in pieces:
        heights = jax.random.uniform(jax.random.fold_in(jax.random.fold_in(rng, 6), axis_at), (shards_of,), jnp.float32, smallest / len(pieces), top_value / len(pieces))
        level = level * jnp.repeat(jnp.exp(heights), shape[axis_at] // shards_of).reshape((-1,) + (1,) * (len(shape) - 1 - axis_at))
    return level


def gaussian(key, shape, width, most, pieces=(), held_as=jnp.bfloat16):
    values = width * jax.random.normal(key, shape, jnp.float32)
    if pieces:
        values = values * steps_of(key, shape, pieces, -0.22, 0.18)
    return jnp.clip(values, -most, most).astype(held_as)


def setup_inputs(seed: int = 0) -> dict:
    splits = jax.random.split(jax.random.key(seed), 15)
    inputs = gaussian(splits[0], (MEMBERS, MICRO, IMGS, SIDE, SIDE, D), 1.0, 6.0, ((0, 32),))
    cotangent = gaussian(splits[1], (MEMBERS, MICRO, IMGS, SIDE, SIDE, D), 1.0, 6.0, ((0, 32),))
    probe = gaussian(splits[2], (MEMBERS, IMGS, SIDE, SIDE, D), 1.0, 6.0, ((0, 32),))
    dw_kernel = gaussian(splits[3], (MEMBERS, SECTIONS, 7, 7, D), 49 ** -0.5, 0.875, ((0, 32), (1, 4)), jnp.float32)
    dw_bias = gaussian(splits[4], (MEMBERS, SECTIONS, D), 0.5, 3.0, ((0, 32), (1, 4)), jnp.float32)
    norm_gain = jnp.clip(1.0 + 0.1 * jax.random.normal(splits[5], (MEMBERS, SECTIONS, D), jnp.float32), 0.5, 1.5)
    norm_bias = gaussian(splits[6], (MEMBERS, SECTIONS, D), 0.5, 3.0, ((0, 32), (1, 4)), jnp.float32)
    w_in = gaussian(splits[7], (MEMBERS, SECTIONS, D, HID), D ** -0.5, 0.25, ((0, 32), (1, 4)), jnp.float32)
    b_in = gaussian(splits[8], (MEMBERS, SECTIONS, HID), 0.5, 3.0, ((0, 32), (1, 4)), jnp.float32)
    w_out = gaussian(splits[9], (MEMBERS, SECTIONS, HID, D), HID ** -0.5, 0.125, ((0, 32), (1, 4)), jnp.float32)
    b_out = gaussian(splits[10], (MEMBERS, SECTIONS, D), 0.5, 3.0, ((0, 32), (1, 4)), jnp.float32)
    layer_scale = jnp.clip(jnp.exp(math.log(1.5) - 1.60943787 * jax.random.uniform(splits[11], (MEMBERS, SECTIONS, D), jnp.float32) ** steps_of(splits[11], (MEMBERS, SECTIONS, D), ((0, 32), (1, 4)), -0.2, 0.2)), 0.3, 1.5)
    shuffle_mask = draw_shuffle_mask(jax.random.fold_in(splits[14], 71), 0)
    source_member = draw_source_member(jax.random.fold_in(splits[14], 71), 0)
    return dict(inputs=inputs, cotangent=cotangent, probe=probe, dw_kernel=dw_kernel, dw_bias=dw_bias, norm_gain=norm_gain, norm_bias=norm_bias, w_in=w_in, b_in=b_in, w_out=w_out, b_out=b_out, layer_scale=layer_scale, shuffle_mask=shuffle_mask, source_member=source_member)


learning_rate = 0.001
norm_epsilon = 1e-06

def block(params, incoming):
    kernel, conv_bias, gain, shift_bias, first_weight, first_bias, second_weight, second_bias, scale = params
    widened = incoming.astype(jnp.float32)
    channels = widened.shape[-1]
    spread = lax.conv_general_dilated(widened, kernel.reshape(kernel.shape[0], kernel.shape[1], 1, channels), (1, 1), 'SAME', dimension_numbers=('NHWC', 'HWIO', 'NHWC'), feature_group_count=channels, precision=lax.Precision.HIGHEST) + conv_bias
    center = lax.optimization_barrier(jnp.mean(spread, axis=-1, keepdims=True))
    offset = spread - center
    variance = lax.optimization_barrier(jnp.mean(offset * offset, axis=-1, keepdims=True))
    normed = (offset * lax.rsqrt(variance + norm_epsilon) * gain + shift_bias).astype(jnp.bfloat16)
    rows = normed.reshape(-1, channels)
    hidden = jax.nn.gelu(jnp.dot(rows, first_weight, preferred_element_type=jnp.float32) + first_bias, approximate=False).astype(jnp.bfloat16)
    mixed = jnp.dot(hidden, second_weight, preferred_element_type=jnp.float32) + second_bias
    return (widened + scale * mixed.reshape(widened.shape)).astype(jnp.bfloat16)

def lowered(params):
    return tuple((leaf.astype(jnp.bfloat16) if position in (4, 6) else leaf for position, leaf in enumerate(params)))

def train_member(member_data):
    images = member_data[0]
    slopes = member_data[1]
    stacked = member_data[2:]
    initials = [tuple((leaf[section] for leaf in stacked)) for section in range(SECTIONS)]
    section_params = [lowered(initial) for initial in initials]
    totals = [tuple((jnp.zeros(leaf.shape, jnp.float32) for leaf in params)) for params in section_params]
    for micro in range(MICRO):
        stored = []
        current = images[micro]
        for section in range(SECTIONS):
            stored.append(current)
            current = block(section_params[section], current)
        slope = slopes[micro]
        for section in reversed(range(SECTIONS)):
            unused, pull = jax.vjp(block, section_params[section], stored[section])
            delta, slope = pull(slope)
            totals[section] = tuple((total + piece.astype(jnp.float32) for total, piece in zip(totals[section], delta)))
    updated = [tuple((leaf - learning_rate * total for leaf, total in zip(initials[section], totals[section]))) for section in range(SECTIONS)]
    return tuple((jnp.stack([updated[section][position] for section in range(SECTIONS)]) for position in range(9)))

def probe_member(member_data):
    current = member_data[0]
    stacked = member_data[1:]
    outputs = []
    for section in range(SECTIONS):
        params = lowered(tuple((leaf[section] for leaf in stacked)))
        current = block(params, current)
        outputs.append(current)
    return jnp.stack(outputs)

def reference(inputs, cotangent, probe, dw_kernel, dw_bias, norm_gain, norm_bias, w_in, b_in, w_out, b_out, layer_scale, shuffle_mask, source_member):
    updated = lax.map(train_member, (inputs, cotangent, dw_kernel, dw_bias, norm_gain, norm_bias, w_in, b_in, w_out, b_out, layer_scale))
    tile_count = HID // TILE
    row_groups = HID // D
    column_tiles = D // TILE
    sources = jnp.transpose(source_member, (2, 0, 1))
    section_index = jnp.arange(SECTIONS, dtype=jnp.int32)
    first_view = updated[4].reshape(MEMBERS, SECTIONS, D, tile_count, TILE)
    moved_first = first_view[sources[:, :, :tile_count], section_index[None, :, None], :, jnp.arange(tile_count, dtype=jnp.int32)[None, None, :], :]
    moved_first = jnp.transpose(moved_first, (0, 1, 3, 2, 4))
    marked_first = shuffle_mask[:, :tile_count][None, :, None, :, None] == 1
    new_first = jnp.where(marked_first, moved_first, first_view).reshape(MEMBERS, SECTIONS, D, HID)
    second_view = updated[6].reshape(MEMBERS, SECTIONS, row_groups, D, column_tiles, TILE)
    second_sources = sources[:, :, tile_count:].reshape(MEMBERS, SECTIONS, column_tiles, row_groups)
    moved_second = second_view[second_sources, section_index[None, :, None, None], jnp.arange(row_groups, dtype=jnp.int32)[None, None, None, :], :, jnp.arange(column_tiles, dtype=jnp.int32)[None, None, :, None], :]
    moved_second = jnp.transpose(moved_second, (0, 1, 3, 4, 2, 5))
    marked_second = jnp.transpose(shuffle_mask[:, tile_count:].reshape(SECTIONS, column_tiles, row_groups), (0, 2, 1))[None, :, :, None, :, None] == 1
    new_second = jnp.where(marked_second, moved_second, second_view).reshape(MEMBERS, SECTIONS, HID, D)
    features = lax.map(probe_member, (probe, updated[0], updated[1], updated[2], updated[3], new_first, updated[5], new_second, updated[7], updated[8]))
    return (new_first, new_second, features)
```

```python
import functools

import jax
import jax.numpy as jnp
from jax import lax
from jax.experimental import pallas as pl
from jax.experimental.pallas import tpu as pltpu
from jax.sharding import PartitionSpec as P

MESH = pl.DeviceIdType.MESH
BF = jnp.bfloat16
F32 = jnp.float32
S = 14
W = 16
R = S * W
D = 512
HID = 2048
LANE = 128
TILE = 128
CH = 512
learning_rate = 0.001
norm_epsilon = 1e-06


def dot(a, b, ca, cb):
    return lax.dot_general(a, b, (((ca,), (cb,)), ((), ())), preferred_element_type=F32)


def loop(n, body):
    lax.fori_loop(0, n, lambda i, c: (body(i), c)[1], 0)


def lanes_of(c):
    return pl.ds(pl.multiple_of(c * LANE, LANE), LANE)


def shifted(x, d):
    col = lax.broadcasted_iota(jnp.int32, (R, LANE), 0) % W + d
    moved = x if d == 0 else pltpu.roll(x, (-d) % R, 0)
    return jnp.where((col >= 0) & (col < S), moved, 0.0).reshape(S, W, LANE)


def fill_shifts(x, sh, lanes):
    for dj in range(7):
        sh[dj, 3 : 3 + S, :, lanes] = shifted(x, dj - 3)


def zero_borders(sh):
    zeros = jnp.zeros((7, 3, W, D), F32)
    sh[:, 0:3] = zeros
    sh[:, 3 + S :] = zeros


def taps(sh, k, lanes, start, flip):
    total = start
    for di in range(7):
        for dj in range(7):
            ki, kj = (6 - di, 6 - dj) if flip else (di, dj)
            weight = k[ki, kj : kj + 1, lanes].reshape(1, 1, LANE)
            total = total + weight * sh[dj, di : di + S, :, lanes]
    return total


def gelu_parts(x):
    t = 1.0 / (1.0 + 0.23164189 * jnp.abs(x))
    e = jnp.exp(-0.5 * (x * x))
    poly = t * (
        0.127414796
        + t * (-0.142248368 + t * (0.7107068705 + t * (-0.7265760135 + t * 0.5307027145)))
    )
    q = poly * e
    return jnp.where(x < 0.0, q, 1.0 - q), e


def forward(x, sh, conv, k, kb, gain, nb, w1, b1, w2, b2, ls, u, h, n, out, keep):
    def conv_lanes(c):
        lanes = lanes_of(c)
        fill_shifts(x[:, :, lanes].reshape(R, LANE), sh, lanes)
        start = jnp.zeros((S, W, LANE), F32) + kb[:, lanes].reshape(1, 1, LANE)
        conv[:, lanes] = taps(sh, k, lanes, start, False).reshape(R, LANE)

    loop(D // LANE, conv_lanes)

    def norm_rows(i):
        rows = pl.ds(pl.multiple_of(i * 32, 32), 32)
        c = conv[rows, :]
        off = c - jnp.mean(c, axis=-1, keepdims=True)
        var = jnp.mean(off * off, axis=-1, keepdims=True)
        rstd = lax.rsqrt(var + norm_epsilon)
        hat = off * rstd
        n[rows, :] = (hat * gain[...] + nb[...]).astype(BF)
        if keep is not None:
            keep[0][rows, :] = hat
            keep[1][rows, :] = rstd

    loop(R // 32, norm_rows)

    for c in range(HID // CH):
        cols = pl.ds(c * CH, CH)
        u[:, cols] = dot(n[...], w1[:, cols], 1, 0)

        def act(i, cols=cols):
            rows = pl.ds(pl.multiple_of(i * 16, 16), 16)
            a = u[rows, cols] + b1[:, cols]
            phi, e = gelu_parts(a)
            h[rows, cols] = (a * phi).astype(BF)
            if keep is not None:
                keep[2][rows, cols] = phi + a * e * 0.3989422804014327

        loop(R // 16, act)
    total = dot(h[...], w2[...], 1, 0)
    mixed = total + b2[...]
    if keep is not None:
        keep[3][...] = mixed
    flat = x[...].reshape(R, D)
    out(flat + ls[...] * mixed)


def unpadded(values):
    col = lax.broadcasted_iota(jnp.int32, (R, D), 0) % W
    return jnp.where(col < S, values, 0.0)


def neighbours_ready():
    s = lax.axis_index("section")
    count = lax.axis_size("section")
    barrier = pltpu.get_barrier_semaphore()
    for other in (lax.rem(s + 1, count), lax.rem(s + count - 1, count)):
        pl.semaphore_signal(barrier, inc=1, device_id={"section": other}, device_id_type=MESH)
    pl.semaphore_wait(barrier, 2)


def to_section(src, dst, send, recv, section):
    return pltpu.make_async_remote_copy(
        src_ref=src,
        dst_ref=dst,
        send_sem=send,
        recv_sem=recv,
        device_id={"section": section},
        device_id_type=MESH,
    )


def train_kernel(
    inputs, cot, k, kb, gain, nb, w1, b1, w2, b2, ls,
    o_k, o_kb, o_gain, o_nb, o_w1, o_b1, o_w2, o_b2, o_ls, o_tiles,
    w1b, w2b, x, sh, shd, conv, xhat, rstd, nrm, u, h, gp, mixed, dmb, du, dc, g,
    gk, gkb, ggain, gnb, gb1, gb2, gls,
    fsend, frecv, bsend, brecv, f_s, f_r, b_s, b_r,
):
    s = lax.axis_index("section")
    last = lax.axis_size("section") - 1
    up = jnp.minimum(s + 1, last)
    down = jnp.maximum(s - 1, 0)
    neighbours_ready()

    def cast(i):
        rows = pl.ds(pl.multiple_of(i * 32, 32), 32)
        w1b[rows, :] = w1[rows, :].astype(BF)
        rows = pl.ds(pl.multiple_of(i * 128, 128), 128)
        w2b[rows, :] = w2[rows, :].astype(BF)

    loop(16, cast)
    for ref in (gk, gkb, ggain, gnb, gb1, gb2, gls):
        ref[...] = jnp.zeros_like(ref)
    for j in range(2):
        zero_borders(sh.at[j])
    zero_borders(shd)

    def take(j, first, given, arrived, wait, dst):
        @pl.when(first)
        def _():
            dst[:, S:W, :] = jnp.zeros((S, W - S, D), F32)
            dst[:, 0:S, :] = given[j].astype(F32)

        @pl.when(jnp.logical_not(first))
        def _():
            wait()
            dst[...] = arrived[j].astype(F32)

    def fwd(j):
        rows = pl.ds(pl.multiple_of(j * R, R), R)
        copy = to_section(fsend.at[j], frecv.at[j], f_s.at[j], f_r.at[j], up)
        take(j, s == 0, inputs, frecv, copy.wait_recv, x.at[j])

        def out(values):
            @pl.when(s < last)
            def _():
                fsend[j] = unpadded(values).astype(BF).reshape(S, W, D)
                copy.start()

        forward(
            x.at[j], sh.at[j], conv, k, kb, gain, nb, w1b, b1, w2b, b2, ls,
            u, h.at[rows, :], nrm.at[rows, :], out,
            (xhat.at[j], rstd.at[j], gp.at[j], mixed.at[j]),
        )

    loop(2, fwd)

    def kernel_grad(j):
        def per_lanes(c):
            lanes = lanes_of(c)
            d = dc[j, :, :, lanes]
            for di in range(7):
                for dj in range(7):
                    prod = jnp.sum(d * sh[j, dj, di : di + S, :, lanes], axis=0)
                    gk[di, dj : dj + 1, lanes] += jnp.sum(prod, axis=0, keepdims=True)

        loop(D // LANE, per_lanes)

    def bwd(j):
        base = pl.multiple_of(j * R, R)
        rows = pl.ds(base, R)
        copy = to_section(bsend.at[j], brecv.at[j], b_s.at[j], b_r.at[j], down)
        take(j, s == last, cot, brecv, copy.wait_recv, g)

        flat = g[...].reshape(R, D)
        dm = flat * ls[...]
        dmb[rows, :] = dm.astype(BF)
        gb2[...] += jnp.sum(dm, axis=0, keepdims=True)
        gls[...] += jnp.sum(flat * mixed[j], axis=0, keepdims=True)
        for c in range(HID // CH):
            cols = pl.ds(c * CH, CH)
            u[:, cols] = dot(dmb[rows, :], w2b[cols, :], 1, 1)

            def act(i, carry, cols=cols):
                r = pl.ds(pl.multiple_of(i * 16, 16), 16)
                a = u[r, cols].astype(BF).astype(F32) * gp[j, r, cols]
                du[pl.ds(pl.multiple_of(base + i * 16, 16), 16), cols] = a.astype(BF)
                return carry + jnp.sum(a.reshape(2, 8, CH), axis=0)

            part = lax.fori_loop(0, R // 16, act, jnp.zeros((8, CH), F32))
            gb1[:, cols] += jnp.sum(part, axis=0, keepdims=True)
        conv[...] = dot(du[rows, :], w1b[...], 1, 1)

        def norm_rows(i, carry):
            r = pl.ds(pl.multiple_of(i * 32, 32), 32)
            dn = conv[r, :].astype(BF).astype(F32)
            hat = xhat[j, r, :]
            dh = dn * gain[...]
            m1 = jnp.mean(dh, axis=-1, keepdims=True)
            m2 = jnp.mean(dh * hat, axis=-1, keepdims=True)
            d = rstd[j, r, :] * (dh - m1 - hat * m2)
            dc[j, pl.ds(i * 2, 2)] = d.reshape(2, W, D)
            a, b, c = carry
            fold = lambda v: jnp.sum(v.reshape(4, 8, D), axis=0)
            return a + fold(dn * hat), b + fold(dn), c + fold(d)

        zero = jnp.zeros((8, D), F32)
        a, b, c = lax.fori_loop(0, R // 32, norm_rows, (zero, zero, zero))
        ggain[...] += jnp.sum(a, axis=0, keepdims=True)
        gnb[...] += jnp.sum(b, axis=0, keepdims=True)
        gkb[...] += jnp.sum(c, axis=0, keepdims=True)

        @pl.when(s > 0)
        def _():
            col = lax.broadcasted_iota(jnp.int32, (S, W, LANE), 1)

            def back_lanes(c):
                lanes = lanes_of(c)
                fill_shifts(dc[j, :, :, lanes].reshape(R, LANE), shd, lanes)
                total = taps(shd, k, lanes, g[:, :, lanes], True)
                bsend[j, :, :, lanes] = jnp.where(col < S, total, 0.0).astype(BF)

            loop(D // LANE, back_lanes)
            copy.start()

        @pl.when((j == 0) & (s < last))
        def _():
            kernel_grad(0)

    loop(2, bwd)
    lax.fori_loop(jnp.where(s == last, 0, 1), 2, lambda j, c: (kernel_grad(j), c)[1], 0)

    def grad_in(c):
        cols = pl.ds(pl.multiple_of(c * 256, 256), 256)
        new = w1[:, cols] - learning_rate * dot(nrm[...], du[:, cols], 0, 0)
        o_w1[:, cols] = new
        for half in range(2):
            o_tiles[2 * c + half] = new[:, half * TILE : (half + 1) * TILE].astype(BF)

    loop(HID // 256, grad_in)

    def grad_out(r):
        rows = pl.ds(pl.multiple_of(r * D, D), D)
        for c in range(2):
            cols = pl.ds(c * 256, 256)
            new = w2[rows, cols] - learning_rate * dot(h[:, rows], dmb[:, cols], 0, 0)
            o_w2[rows, cols] = new
            for half in range(2):
                o_tiles[16 + (2 * c + half) * 4 + r] = new[:, half * TILE : (half + 1) * TILE].astype(BF)

    loop(HID // D, grad_out)

    for old, grad, new in (
        (k, gk, o_k), (kb, gkb, o_kb), (gain, ggain, o_gain), (nb, gnb, o_nb),
        (b1, gb1, o_b1), (b2, gb2, o_b2), (ls, gls, o_ls),
    ):
        new[...] = old[...] - learning_rate * grad[...]

    for j in range(2):

        @pl.when(s < last)
        def _(j=j):
            to_section(fsend.at[j], frecv.at[j], f_s.at[j], f_r.at[j], up).wait_send()

        @pl.when(s > 0)
        def _(j=j):
            to_section(bsend.at[j], brecv.at[j], b_s.at[j], b_r.at[j], down).wait_send()


def vmem(n):
    return [pl.BlockSpec(memory_space=pltpu.VMEM)] * n


def params(collective, mib=60):
    return pltpu.CompilerParams(
        collective_id=collective, has_side_effects=True, vmem_limit_bytes=mib * 2**20
    )


def train(inputs, cot, small, w1, w2):
    k, kb, gain, nb, b1, b2, ls = small
    row = jax.ShapeDtypeStruct((1, D), F32)
    dma = pltpu.SemaphoreType.DMA
    V = pltpu.VMEM
    wide = (2, S, W, D)
    return pl.pallas_call(
        train_kernel,
        out_shape=(
            jax.ShapeDtypeStruct((7, 7, D), F32), row, row, row,
            jax.ShapeDtypeStruct((D, HID), F32), jax.ShapeDtypeStruct((1, HID), F32),
            jax.ShapeDtypeStruct((HID, D), F32), row, row,
            jax.ShapeDtypeStruct((32, D, TILE), BF),
        ),
        in_specs=vmem(11),
        out_specs=vmem(10),
        scratch_shapes=[
            V((D, HID), BF), V((HID, D), BF), V(wide, F32), V((2, 7, S + 6, W, D), F32),
            V((7, S + 6, W, D), F32), V((R, D), F32), V((2, R, D), F32), V((2, R, 1), F32),
            V((2 * R, D), BF), V((R, HID), F32), V((2 * R, HID), BF), V((2, R, HID), F32),
            V((2, R, D), F32), V((2 * R, D), BF), V((2 * R, HID), BF), V(wide, F32),
            V((S, W, D), F32),
            V((7, 7, D), F32), V((1, D), F32), V((1, D), F32), V((1, D), F32),
            V((1, HID), F32), V((1, D), F32), V((1, D), F32),
            V(wide, BF), V(wide, BF), V(wide, BF), V(wide, BF),
            dma((2,)), dma((2,)), dma((2,)), dma((2,)),
        ],
        compiler_params=params(0),
        name="train",
    )(inputs, cot, k, kb, gain, nb, w1, b1, w2, b2, ls)


def exchange_kernel(block_of, slot_of, marked, tiles, o_w1, o_w2, outgoing, incoming, send, recv):
    me = lax.axis_index("member")
    members = lax.axis_size("member")
    barrier = pltpu.get_barrier_semaphore()

    def greet(t):
        pl.semaphore_signal(
            barrier, inc=1, device_id={"member": lax.rem(me + t, members)}, device_id_type=MESH
        )

    lax.fori_loop(1, members, lambda t, c: (greet(t), c)[1], 0)
    pl.semaphore_wait(barrier, members - 1)

    def copy(t):
        return pltpu.make_async_remote_copy(
            src_ref=outgoing.at[t],
            dst_ref=incoming.at[t],
            send_sem=send.at[t],
            recv_sem=recv.at[t],
            device_id={"member": lax.rem(me + t, members)},
            device_id_type=MESH,
        )

    def push(t):
        outgoing[t] = tiles[block_of[t]]
        copy(t).start()

    lax.fori_loop(1, members, lambda t, c: (push(t), c)[1], 0)
    lax.fori_loop(1, members, lambda t, c: (copy(t).wait_recv(), c)[1], 0)

    def chosen(b):
        return jnp.where(marked[b] == 1, incoming[slot_of[b]], tiles[b])

    def place_in(b):
        o_w1[:, lanes_of(b)] = chosen(b)

    loop(16, place_in)

    def place_out(r):
        for c in range(4):
            o_w2[pl.ds(pl.multiple_of(r * D, D), D), pl.ds(c * TILE, TILE)] = chosen(16 + 4 * c + r)

    loop(4, place_out)
    lax.fori_loop(1, members, lambda t, c: (copy(t).wait_send(), c)[1], 0)


def exchange(tiles, block_of, slot_of, marked):
    smem = pl.BlockSpec(memory_space=pltpu.SMEM)
    dma = pltpu.SemaphoreType.DMA
    return pl.pallas_call(
        exchange_kernel,
        out_shape=(jax.ShapeDtypeStruct((D, HID), BF), jax.ShapeDtypeStruct((HID, D), BF)),
        in_specs=[smem, smem, smem] + vmem(1),
        out_specs=vmem(2),
        scratch_shapes=[
            pltpu.VMEM((32, D, TILE), BF), pltpu.VMEM((32, D, TILE), BF), dma((32,)), dma((32,)),
        ],
        compiler_params=params(1, 24),
        name="exchange",
    )(block_of, slot_of, marked, tiles)


def probe_kernel(
    probe, k, kb, gain, nb, w1, b1, w2, b2, ls,
    out_ref,
    x, sh, conv, nrm, u, h, fsend, frecv, f_s, f_r,
):
    s = lax.axis_index("section")
    last = lax.axis_size("section") - 1
    up = jnp.minimum(s + 1, last)
    neighbours_ready()
    zero_borders(sh)
    copy = to_section(fsend, frecv, f_s, f_r, up)

    @pl.when(s == 0)
    def _():
        x[:, S:W, :] = jnp.zeros((S, W - S, D), F32)
        x[:, 0:S, :] = probe[...].astype(F32)

    @pl.when(s > 0)
    def _():
        copy.wait_recv()
        x[...] = frecv[...].astype(F32)

    def out(values):
        fsend[...] = unpadded(values).astype(BF).reshape(S, W, D)

        @pl.when(s < last)
        def _():
            copy.start()

        out_ref[...] = fsend[:, 0:S, :]

    forward(x, sh, conv, k, kb, gain, nb, w1, b1, w2, b2, ls, u, h, nrm, out, None)

    @pl.when(s < last)
    def _():
        copy.wait_send()


def run_probe(probe, small, w1, w2):
    k, kb, gain, nb, b1, b2, ls = small
    dma = pltpu.SemaphoreType.DMA
    V = pltpu.VMEM
    return pl.pallas_call(
        probe_kernel,
        out_shape=jax.ShapeDtypeStruct((S, S, D), BF),
        in_specs=vmem(10),
        out_specs=vmem(1)[0],
        scratch_shapes=[
            V((S, W, D), F32), V((7, S + 6, W, D), F32), V((R, D), F32), V((R, D), BF),
            V((R, HID), F32), V((R, HID), BF), V((S, W, D), BF), V((S, W, D), BF), dma, dma,
        ],
        compiler_params=params(2, 30),
        name="probe",
    )(probe, k, kb, gain, nb, w1, b1, w2, b2, ls)


def local(
    inputs, cotangent, probe, dw_kernel, dw_bias, norm_gain, norm_bias, w_in, b_in, w_out, b_out,
    layer_scale, shuffle_mask, source_member,
):
    member = lax.axis_index("member")
    members = lax.axis_size("member")
    small = (
        dw_kernel[0, 0], dw_bias[0], norm_gain[0], norm_bias[0], b_in[0], b_out[0], layer_scale[0],
    )
    sources, marked = source_member[0], shuffle_mask[0]
    ids = jnp.arange(32, dtype=jnp.int32)
    block_for = jnp.sum(
        jnp.where((sources == member) & (marked == 1)[:, None], ids[:, None], 0), axis=0
    )
    block_of = jnp.roll(block_for, -member)
    mine = lax.dynamic_index_in_dim(sources, member, axis=1, keepdims=False)
    slot_of = (member - mine + members) % members

    res = train(inputs[0, :, 0], cotangent[0, :, 0], small, w_in[0, 0], w_out[0, 0])
    o_k, o_kb, o_gain, o_nb, u_w1, o_b1, u_w2, o_b2, o_ls, tiles = res
    w1b, w2b = exchange(tiles, block_of, slot_of, marked)
    out = run_probe(probe[0, 0], (o_k, o_kb, o_gain, o_nb, o_b1, o_b2, o_ls), w1b, w2b)

    is_in = jnp.repeat(marked[:16], TILE)[None, :] == 1
    is_out = jnp.repeat(jnp.repeat(marked[16:].reshape(4, 4).T, D, axis=0), TILE, axis=1) == 1
    new_in = jnp.where(is_in, w1b.astype(F32), u_w1)
    new_out = jnp.where(is_out, w2b.astype(F32), u_w2)
    return new_in[None, None], new_out[None, None], out[None, None, None]


def solution(mesh):
    return jax.shard_map(
        local,
        mesh=mesh,
        in_specs=(
            P("member", None, None, None, None, None),
            P("member", None, None, None, None, None),
            P("member", None, None, None, None),
            P("member", "section", None, None, None),
            P("member", "section", None),
            P("member", "section", None),
            P("member", "section", None),
            P("member", "section", None, None),
            P("member", "section", None),
            P("member", "section", None, None),
            P("member", "section", None),
            P("member", "section", None),
            P("section", None),
            P("section", None, None),
        ),
        out_specs=(
            P("member", "section", None, None),
            P("member", "section", None, None),
            P("member", "section", None, None, None, None),
        ),
        check_vma=False,
    )
```

```python
import jax
import jax.numpy as jnp
from jax import lax
from jax.experimental import pallas as pl
from jax.experimental.pallas import tpu as pltpu
from jax.sharding import PartitionSpec as P

MESH = pl.DeviceIdType.MESH
BF = jnp.bfloat16
F32 = jnp.float32
S = 14
W = 16
R = S * W
HS, HR = S // 2, R // 2
D = 512
HID = 2048
LANE = 128
TILE = 128
CH = 256
learning_rate = 0.001
norm_epsilon = 1e-06

CHIPS = (
    (0, 0), (0, 1), (1, 0), (0, 3), (3, 0), (1, 1), (3, 3), (1, 3), (3, 1),
    (0, 2), (2, 0), (2, 2), (1, 2), (2, 1), (3, 2), (2, 3),
)
ORDER = tuple(z * 8 + x * 2 + c for c in (1, 0) for z, x in CHIPS if (z, x, c) != (0, 0, 0))


def at_distance(me, t, sign=1):
    z = lax.rem(me // 8 + sign * (t // 8) + 4, 4)
    x = lax.rem(lax.rem(me // 2, 4) + sign * (t // 2 % 4) + 4, 4)
    c = lax.rem(lax.rem(me, 2) + t % 2, 2)
    return z * 8 + x * 2 + c


def dot(a, b, ca, cb):
    return lax.dot_general(a, b, (((ca,), (cb,)), ((), ())), preferred_element_type=F32)


def loop(n, body):
    lax.fori_loop(0, n, lambda i, c: (body(i), c)[1], 0)


def lanes_of(c):
    return pl.ds(pl.multiple_of(c * LANE, LANE), LANE)


def half_rows(half, base=0):
    return pl.ds(pl.multiple_of(base + half * HR, HR), HR)


def conv_half(src, sh, k, total, start, half, flip):
    base = half * HS
    rows = range(0, HS + 3) if half == 0 else range(HS - 3, S)
    begun = () if half == 0 else range(HS - 3, HS + 3)

    def per_lanes(c):
        lanes = lanes_of(c)
        v = src[base : base + HS, :, lanes]
        col = lax.broadcasted_iota(jnp.int32, (HS, W, LANE), 1)
        for dj in range(7):
            d = dj - 3
            moved = v if d == 0 else pltpu.roll(v, (-d) % W, 1)
            sh[dj, base : base + HS, :, lanes] = jnp.where((col + d >= 0) & (col + d < S), moved, 0.0)
        acc = {r: total[r, :, lanes] if r in begun else start(r, lanes) for r in rows}
        for dj in range(7):
            ks = [k[6 - di, 6 - dj, :, lanes] if flip else k[di, dj, :, lanes] for di in range(7)]
            for i in range(base, base + HS):
                x = sh[dj, i, :, lanes]
                for r in rows:
                    if abs(r - i) <= 3:
                        acc[r] = acc[r] + ks[i - r + 3] * x
        for r in rows:
            total[r, :, lanes] = acc[r]

    loop(D // LANE, per_lanes)


def gelu_parts(x):
    t = 1.0 / (1.0 + 0.23164189 * jnp.abs(x))
    e = jnp.exp(-0.5 * (x * x))
    poly = t * (
        0.127414796
        + t * (-0.142248368 + t * (0.7107068705 + t * (-0.7265760135 + t * 0.5307027145)))
    )
    q = poly * e
    return jnp.where(x < 0.0, q, 1.0 - q), e


def forward(take, x, sh, conv, k, kb, gain, nb, w1, b1, w2, b2, ls, h, n, give, before, keep):
    def bias(r, lanes):
        return jnp.broadcast_to(kb[:, lanes], (W, LANE))

    for half in range(2):
        take(half)
        conv_half(x, sh, k, conv, bias, half, False)
    before()
    for half in range(2):
        rows = slice(half * HR, half * HR + HR)
        c = conv[half * HS : half * HS + HS].reshape(HR, D)
        off = c - jnp.mean(c, axis=-1, keepdims=True)
        var = jnp.mean(off * off, axis=-1, keepdims=True)
        rstd = lax.rsqrt(var + norm_epsilon)
        hat = off * rstd
        n[rows, :] = (hat * gain[...] + nb[...]).astype(BF)
        if keep is not None:
            keep[0][rows, :] = hat
            keep[1][rows, :] = rstd
        for c in range(HID // CH):
            cols = slice(c * CH, c * CH + CH)
            a = dot(n[rows, :], w1[:, cols], 1, 0) + b1[:, cols]
            phi, e = gelu_parts(a)
            h[rows, cols] = (a * phi).astype(BF)
            if keep is not None:
                keep[2][rows, cols] = phi + a * e * 0.3989422804014327
        mixed = dot(h[rows, :], w2[...], 1, 0) + b2[...]
        if keep is not None:
            keep[3][rows, :] = mixed
        give(half, x[half * HS : half * HS + HS].reshape(HR, D) + ls[...] * mixed)


def unpadded(values):
    col = lax.broadcasted_iota(jnp.int32, values.shape, 1)
    return jnp.where(col < S, values, 0.0)


def to_section(src, dst, send, recv, section):
    return pltpu.make_async_remote_copy(
        src_ref=src,
        dst_ref=dst,
        send_sem=send,
        recv_sem=recv,
        device_id={"section": section},
        device_id_type=MESH,
    )


def greet_sections(barrier):
    s = lax.axis_index("section")
    count = lax.axis_size("section")
    for other in (lax.rem(s + 1, count), lax.rem(s + count - 1, count)):
        pl.semaphore_signal(barrier, inc=1, device_id={"section": other}, device_id_type=MESH)


def train_kernel(
    sources, marked,
    inputs, cot, k, kb, gain, nb, w1, b1, w2, b2, ls,
    o_w1, o_w2, o_s1, o_s2, o_k, o_kb, o_gain, o_nb, o_b1, o_b2, o_ls,
    w1f, w2f, w1b, w2b, x, sh, shd, conv, xhat, rstd, nrm, h, gp, mixed, dmb, du, dc, g,
    pt, gkb, ggain, gnb, gb1, gb2, gls, tiles, outgoing, incoming,
    fsend, frecv, bsend, brecv, f_s, f_r, b_s, b_r, w_in, w_out, e_s, e_r, block_of,
):
    s = lax.axis_index("section")
    last = lax.axis_size("section") - 1
    up = jnp.minimum(s + 1, last)
    down = jnp.maximum(s - 1, 0)
    me = lax.axis_index("member")

    loads = [
        pltpu.make_async_copy(w1, w1f, w_in.at[0]),
        pltpu.make_async_copy(w2, w2f, w_in.at[1]),
    ]
    for load in loads:
        load.start()
    barrier = pltpu.get_barrier_semaphore()
    greet_sections(barrier)
    for t in ORDER:
        pl.semaphore_signal(
            barrier, inc=1, device_id={"member": at_distance(me, t)}, device_id_type=MESH
        )
    for ref in (pt, gkb, ggain, gnb, gb1, gb2, gls):
        ref[...] = jnp.zeros_like(ref)
    pl.semaphore_wait(barrier, 2 + len(ORDER))

    def tables():
        def per_slot(t):
            to = at_distance(me, t)
            block = jnp.int32(0)
            for b in range(32):
                block = jnp.where((sources[b, to] == me) & (marked[b] == 1), b, block)
            block_of[t] = block

        loop(32, per_slot)

    @pl.when(s > 0)
    def _():
        tables()

    def take(half, first, given, arrived, wait, dst):
        rows = slice(half * HS, half * HS + HS)

        @pl.when(first)
        def _():
            dst[rows, S:W, :] = jnp.zeros((HS, W - S, D), F32)
            dst[rows, 0:S, :] = given[rows].astype(F32)

        @pl.when(jnp.logical_not(first))
        def _():
            wait()
            dst[rows] = arrived[rows].astype(F32)

    def half_copy(send, recv, sems, j, half, section):
        rows = pl.ds(half * HS, HS)
        return to_section(
            send.at[j, rows], recv.at[j, rows], sems[0].at[j, half], sems[1].at[j, half], section
        )

    def fwd_copy(j, half):
        return half_copy(fsend, frecv, (f_s, f_r), j, half, up)

    def bwd_copy(j, half):
        return half_copy(bsend, brecv, (b_s, b_r), j, half, down)

    def fwd(j):
        rows = pl.ds(pl.multiple_of(j * R, R), R)

        def before():
            @pl.when(j == 0)
            def _():
                for load in loads:
                    load.wait()

                def cast(i):
                    r = pl.ds(pl.multiple_of(i * 32, 32), 32)
                    w1b[r, :] = w1f[r, :].astype(BF)
                    r = pl.ds(pl.multiple_of(i * 128, 128), 128)
                    w2b[r, :] = w2f[r, :].astype(BF)

                loop(16, cast)

        def give(half, values):
            @pl.when(s < last)
            def _():
                fsend[j, half * HS : half * HS + HS] = unpadded(values.reshape(HS, W, D)).astype(BF)
                fwd_copy(j, half).start()

        forward(
            lambda half: take(
                half, s == 0, inputs.at[j], frecv.at[j], fwd_copy(j, half).wait_recv, x.at[j]
            ),
            x.at[j], sh.at[j], conv, k, kb, gain, nb, w1b, b1, w2b, b2, ls,
            h.at[rows, :], nrm.at[rows, :], give, before,
            (xhat.at[j], rstd.at[j], gp.at[j], mixed.at[j]),
        )

    loop(2, fwd)

    @pl.when(s == 0)
    def _():
        tables()

    def kernel_grad(j):
        def per_lanes(c):
            lanes = lanes_of(c)
            for dj in range(7):
                acc = [None] * 7
                for r in range(S):
                    d = dc[j, r, :, lanes]
                    for di in range(7):
                        if 0 <= r + di - 3 < S:
                            p = d * sh[j, dj, r + di - 3, :, lanes]
                            acc[di] = p if acc[di] is None else acc[di] + p
                for di in range(7):
                    pt[di, dj, :, lanes] += acc[di][0:8] + acc[di][8:16]

        loop(D // LANE, per_lanes)

    def bwd(j):
        def nothing(r, lanes):
            return jnp.zeros((W, LANE), F32)

        for half in range(2):
            base = pl.multiple_of(j * R, R)
            rows = slice(half * HR, half * HR + HR)
            both = half_rows(half, base)
            take(half, s == last, cot.at[j], brecv.at[j], bwd_copy(j, half).wait_recv, g)
            flat = g[half * HS : half * HS + HS].reshape(HR, D)
            dm = flat * ls[...]
            dmb[both, :] = dm.astype(BF)
            gb2[...] += jnp.sum(dm, axis=0, keepdims=True)
            gls[...] += jnp.sum(flat * mixed[j, rows, :], axis=0, keepdims=True)
            for c in range(HID // CH):
                cols = slice(c * CH, c * CH + CH)
                a = dot(dmb[both, :], w2b[cols, :], 1, 1) * gp[j, rows, cols]
                du[both, cols] = a.astype(BF)
                gb1[:, cols] += jnp.sum(a, axis=0, keepdims=True)
            dn = dot(du[both, :], w1b[...], 1, 1)
            hat = xhat[j, rows, :]
            dh = dn * gain[...]
            m1 = jnp.mean(dh, axis=-1, keepdims=True)
            m2 = jnp.mean(dh * hat, axis=-1, keepdims=True)
            d = rstd[j, rows, :] * (dh - m1 - hat * m2)
            dc[j, half * HS : half * HS + HS] = d.reshape(HS, W, D)
            ggain[...] += jnp.sum(dn * hat, axis=0, keepdims=True)
            gnb[...] += jnp.sum(dn, axis=0, keepdims=True)
            gkb[...] += jnp.sum(d, axis=0, keepdims=True)

            @pl.when(s > 0)
            def _(half=half):
                conv_half(dc.at[j], shd, k, conv, nothing, half, True)

        @pl.when(s > 0)
        def _():
            for half in range(2):
                part = slice(half * HS, half * HS + HS)
                bsend[j, part] = unpadded(g[part] + conv[part]).astype(BF)
                bwd_copy(j, half).start()

        @pl.when((j == 0) & (s < last))
        def _():
            kernel_grad(0)

    loop(2, bwd)

    stores = []

    def store(src, dst):
        copy = pltpu.make_async_copy(src, dst, w_out.at[len(stores)])
        copy.start()
        stores.append(copy)

    for c in range(4):
        cols = pl.ds(c * 512, 512)
        new = w1f[:, cols] - learning_rate * dot(nrm[...], du[:, cols], 0, 0)
        w1f[:, cols] = new
        for q in range(4):
            tiles[4 * c + q] = new[:, q * TILE : (q + 1) * TILE].astype(BF)
    for r in range(HID // D):
        rows = pl.ds(r * D, D)
        new = w2f[rows, :] - learning_rate * dot(h[:, rows], dmb[...], 0, 0)
        w2f[rows, :] = new
        for q in range(4):
            tiles[16 + 4 * q + r] = new[:, q * TILE : (q + 1) * TILE].astype(BF)

    def push_copy(t):
        return pltpu.make_async_remote_copy(
            src_ref=outgoing.at[t],
            dst_ref=incoming.at[t],
            send_sem=e_s.at[t],
            recv_sem=e_r.at[t],
            device_id={"member": at_distance(me, t)},
            device_id_type=MESH,
        )

    for t in ORDER:
        outgoing[t] = tiles[block_of[t]]
        push_copy(t).start()

    store(w1f, o_w1)
    store(w2f, o_w2)
    lax.fori_loop(jnp.where(s == last, 0, 1), 2, lambda j, c: (kernel_grad(j), c)[1], 0)
    for di in range(7):
        for dj in range(7):
            o_k[di, dj] = k[di, dj] - learning_rate * jnp.sum(pt[di, dj], axis=0, keepdims=True)
    for old, grad, new in (
        (kb, gkb, o_kb), (gain, ggain, o_gain), (nb, gnb, o_nb),
        (b1, gb1, o_b1), (b2, gb2, o_b2), (ls, gls, o_ls),
    ):
        new[...] = old[...] - learning_rate * grad[...]

    for t in ORDER:
        push_copy(t).wait_recv()

    def chosen(b):
        source = sources[b, me]
        z = lax.rem(me // 8 - source // 8 + 4, 4)
        x = lax.rem(lax.rem(me // 2, 4) - lax.rem(source // 2, 4) + 4, 4)
        c = lax.rem(lax.rem(me, 2) + lax.rem(source, 2), 2)
        return jnp.where(marked[b] == 1, incoming[z * 8 + x * 2 + c], tiles[b])

    def place_in(b):
        w1b[:, lanes_of(b)] = chosen(b)

    loop(16, place_in)
    store(w1b, o_s1)

    def place_out(r):
        for c in range(4):
            w2b[pl.ds(pl.multiple_of(r * D, D), D), pl.ds(c * TILE, TILE)] = chosen(16 + 4 * c + r)

    loop(4, place_out)
    store(w2b, o_s2)

    for copy in stores:
        copy.wait()
    for t in ORDER:
        push_copy(t).wait_send()
    for j in range(2):
        for half in range(2):

            @pl.when(s < last)
            def _(j=j, half=half):
                fwd_copy(j, half).wait_send()

            @pl.when(s > 0)
            def _(j=j, half=half):
                bwd_copy(j, half).wait_send()


def vmem(n):
    return [pl.BlockSpec(memory_space=pltpu.VMEM)] * n


def hbm(n):
    return [pl.BlockSpec(memory_space=pltpu.HBM)] * n


def params(collective, mib):
    return pltpu.CompilerParams(
        collective_id=collective, has_side_effects=True, vmem_limit_bytes=mib * 2**20
    )


def train(tables, inputs, cot, small, w1, w2):
    k, kb, gain, nb, b1, b2, ls = small
    dma = pltpu.SemaphoreType.DMA
    V = pltpu.VMEM
    shape = jax.ShapeDtypeStruct
    row = shape((1, D), F32)
    wide = (2, S, W, D)
    return pl.pallas_call(
        train_kernel,
        out_shape=(
            shape((D, HID), F32), shape((HID, D), F32), shape((D, HID), BF), shape((HID, D), BF),
            shape((7, 7, 1, D), F32), row, row, row, shape((1, HID), F32), row, row,
        ),
        in_specs=[pl.BlockSpec(memory_space=pltpu.SMEM)] * 2 + vmem(6) + hbm(1) + vmem(1) + hbm(1) + vmem(2),
        out_specs=hbm(4) + vmem(7),
        scratch_shapes=[
            V((D, HID), F32), V((HID, D), F32), V((D, HID), BF), V((HID, D), BF),
            V(wide, F32), V((2, 7, S, W, D), F32), V((7, S, W, D), F32), V((S, W, D), F32),
            V((2, R, D), F32), V((2, R, 1), F32), V((2 * R, D), BF), V((2 * R, HID), BF),
            V((2, R, HID), F32), V((2, R, D), F32), V((2 * R, D), BF), V((2 * R, HID), BF),
            V(wide, F32), V((S, W, D), F32),
            V((7, 7, 8, D), F32), V((1, D), F32), V((1, D), F32), V((1, D), F32),
            V((1, HID), F32), V((1, D), F32), V((1, D), F32),
            V((32, D, TILE), BF), V((32, D, TILE), BF), V((32, D, TILE), BF),
            V(wide, BF), V(wide, BF), V(wide, BF), V(wide, BF),
            dma((2, 2)), dma((2, 2)), dma((2, 2)), dma((2, 2)), dma((2,)), dma((4,)),
            dma((32,)), dma((32,)), pltpu.SMEM((32,), jnp.int32),
        ],
        compiler_params=params(0, 60),
        name="train",
    )(*tables, inputs, cot, k, kb, gain, nb, w1, b1, w2, b2, ls)


def probe_kernel(
    probe, k, kb, gain, nb, w1_hbm, b1, w2_hbm, b2, ls, after,
    out_ref,
    w1, w2, x, sh, conv, nrm, h, fsend, frecv, f_s, f_r, w_in,
):
    s = lax.axis_index("section")
    last = lax.axis_size("section") - 1
    up = jnp.minimum(s + 1, last)
    loads = [
        pltpu.make_async_copy(w1_hbm, w1, w_in.at[0]),
        pltpu.make_async_copy(w2_hbm, w2, w_in.at[1]),
    ]
    for load in loads:
        load.start()
    barrier = pltpu.get_barrier_semaphore()
    greet_sections(barrier)
    pl.semaphore_wait(barrier, 2)

    def loaded():
        for load in loads:
            load.wait()

    def copy(half):
        rows = pl.ds(half * HS, HS)
        return to_section(fsend.at[rows], frecv.at[rows], f_s.at[half], f_r.at[half], up)

    def take(half):
        rows = slice(half * HS, half * HS + HS)

        @pl.when(s == 0)
        def _():
            x[rows, S:W, :] = jnp.zeros((HS, W - S, D), F32)
            x[rows, 0:S, :] = probe[rows].astype(F32)

        @pl.when(s > 0)
        def _():
            copy(half).wait_recv()
            x[rows] = frecv[rows].astype(F32)

    def give(half, values):
        rows = slice(half * HS, half * HS + HS)
        fsend[rows] = unpadded(values.reshape(HS, W, D)).astype(BF)

        @pl.when(s < last)
        def _():
            copy(half).start()

        out_ref[rows] = fsend[rows, 0:S, :]

    forward(
        take, x, sh, conv, k, kb, gain, nb, w1, b1, w2, b2, ls, h, nrm, give, loaded, None
    )

    @pl.when(s < last)
    def _():
        for half in range(2):
            copy(half).wait_send()


def run_probe(probe, small, w1, w2, after):
    k, kb, gain, nb, b1, b2, ls = small
    dma = pltpu.SemaphoreType.DMA
    V = pltpu.VMEM
    return pl.pallas_call(
        probe_kernel,
        out_shape=jax.ShapeDtypeStruct((S, S, D), BF),
        in_specs=vmem(5) + hbm(1) + vmem(1) + hbm(1) + vmem(2) + hbm(1),
        out_specs=vmem(1)[0],
        scratch_shapes=[
            V((D, HID), BF), V((HID, D), BF), V((S, W, D), F32), V((7, S, W, D), F32), V((S, W, D), F32), V((R, D), BF),
            V((R, HID), BF), V((S, W, D), BF), V((S, W, D), BF), dma((2,)), dma((2,)), dma((2,)),
        ],
        compiler_params=params(1, 24),
        name="probe",
    )(probe, k, kb, gain, nb, w1, b1, w2, b2, ls, after)


PARTS = 8


def finish_kernel(first, *refs):
    if first:
        marked, u1, u2, s1, s2, o1, o2, f1, f2, b1, b2, sem, out = refs
    else:
        marked, u1, u2, s1, s2, _, _, _, o1, o2, f1, f2, b1, b2, sem, out = refs
    s = lax.axis_index("section")

    @pl.when(s > 0 if first else s == 0)
    def _():
        def rows_of(i):
            return pl.ds(i * (D // PARTS), D // PARTS), pl.ds(i * (HID // PARTS), HID // PARTS)

        ins, outs = [], []
        for i in range(PARTS):
            r1, r2 = rows_of(i)
            pairs = ((u1, f1, r1), (u2, f2, r2), (s1, b1, r1), (s2, b2, r2))
            ins.append(
                [
                    pltpu.make_async_copy(a.at[r, :], b.at[r, :], sem.at[i, q])
                    for q, (a, b, r) in enumerate(pairs)
                ]
            )
            outs.append(
                [
                    pltpu.make_async_copy(a.at[r, :], b.at[r, :], out.at[i, q])
                    for q, (a, b, r) in enumerate(((f1, o1, r1), (f2, o2, r2)))
                ]
            )
        for part in ins:
            for copy in part:
                copy.start()
        for i in range(PARTS):
            r1, r2 = rows_of(i)
            for copy in ins[i]:
                copy.wait()
            for c in range(16):
                at = (r1, pl.ds(c * TILE, TILE))
                f1[at] = jnp.where(marked[c] == 1, b1[at].astype(F32), f1[at])
            outs[i][0].start()
            for c in range(4):
                at = (r2, pl.ds(c * TILE, TILE))
                b = 16 + 4 * c + i // (PARTS // 4)
                f2[at] = jnp.where(marked[b] == 1, b2[at].astype(F32), f2[at])
            outs[i][1].start()
        for part in outs:
            for copy in part:
                copy.wait()


def finish(marked, weights, earlier):
    dma = pltpu.SemaphoreType.DMA
    V = pltpu.VMEM
    first = not earlier
    return pl.pallas_call(
        lambda *refs: finish_kernel(first, *refs),
        out_shape=(jax.ShapeDtypeStruct((D, HID), F32), jax.ShapeDtypeStruct((HID, D), F32)),
        in_specs=[pl.BlockSpec(memory_space=pltpu.SMEM)] + hbm(4 + len(earlier)),
        out_specs=hbm(2),
        scratch_shapes=[
            V((D, HID), F32), V((HID, D), F32), V((D, HID), BF), V((HID, D), BF),
            dma((PARTS, 4)), dma((PARTS, 2)),
        ],
        input_output_aliases={} if first else {5: 0, 6: 1},
        compiler_params=pltpu.CompilerParams(vmem_limit_bytes=24 * 2**20),
        name="finish" if first else "finish_zero",
    )(marked, *weights, *earlier)


def local(
    inputs, cotangent, probe, dw_kernel, dw_bias, norm_gain, norm_bias, w_in, b_in, w_out, b_out,
    layer_scale, shuffle_mask, source_member,
):
    small = (
        dw_kernel[0, 0][:, :, None, :], dw_bias[0], norm_gain[0], norm_bias[0], b_in[0], b_out[0],
        layer_scale[0],
    )
    marked = shuffle_mask[0]
    res = train(
        (source_member[0], marked), inputs[0, :, 0], cotangent[0, :, 0], small, w_in[0, 0], w_out[0, 0]
    )
    weights, fresh = res[:4], res[4:]
    earlier = finish(marked, weights, ())
    out = run_probe(probe[0, 0], fresh, weights[2], weights[3], earlier[0])
    new_in, new_out = finish(marked, weights, (*earlier, out))
    return new_in[None, None], new_out[None, None], out[None, None, None]


def solution(mesh):
    return jax.shard_map(
        local,
        mesh=mesh,
        in_specs=(
            P("member", None, None, None, None, None),
            P("member", None, None, None, None, None),
            P("member", None, None, None, None),
            P("member", "section", None, None, None),
            P("member", "section", None),
            P("member", "section", None),
            P("member", "section", None),
            P("member", "section", None, None),
            P("member", "section", None),
            P("member", "section", None, None),
            P("member", "section", None),
            P("member", "section", None),
            P("section", None),
            P("section", None, None),
        ),
        out_specs=(
            P("member", "section", None, None),
            P("member", "section", None, None),
            P("member", "section", None, None, None, None),
        ),
        check_vma=False,
    )
```

```python
import jax
import jax.numpy as jnp
from jax import lax
from jax.experimental import pallas as pl
from jax.experimental.pallas import tpu as pltpu
from jax.sharding import PartitionSpec as P

MESH = pl.DeviceIdType.MESH
BF = jnp.bfloat16
F32 = jnp.float32
S = 14
W = 16
R = S * W
HS, HR = S // 2, R // 2
D = 512
HID = 2048
LANE = 128
TILE = 128
CH = 256
learning_rate = 0.001
norm_epsilon = 1e-06

CHIPS = (
    (0, 0), (0, 1), (1, 0), (0, 3), (3, 0), (1, 1), (3, 3), (1, 3), (3, 1),
    (0, 2), (2, 0), (2, 2), (1, 2), (2, 1), (3, 2), (2, 3),
)
ORDER = tuple(z * 8 + x * 2 + c for c in (1, 0) for z, x in CHIPS if (z, x, c) != (0, 0, 0))


def at_distance(me, t, sign=1):
    z = lax.rem(me // 8 + sign * (t // 8) + 4, 4)
    x = lax.rem(lax.rem(me // 2, 4) + sign * (t // 2 % 4) + 4, 4)
    c = lax.rem(lax.rem(me, 2) + t % 2, 2)
    return z * 8 + x * 2 + c


def dot(a, b, ca, cb):
    return lax.dot_general(a, b, (((ca,), (cb,)), ((), ())), preferred_element_type=F32)


def loop(n, body):
    lax.fori_loop(0, n, lambda i, c: (body(i), c)[1], 0)


def lanes_of(c):
    return pl.ds(pl.multiple_of(c * LANE, LANE), LANE)


def half_rows(half, base=0):
    return pl.ds(pl.multiple_of(base + half * HR, HR), HR)


def conv_half(src, sh, k, total, start, half, flip):
    base = half * HS
    rows = range(0, HS + 3) if half == 0 else range(HS - 3, S)
    begun = () if half == 0 else range(HS - 3, HS + 3)

    def per_lanes(c):
        lanes = lanes_of(c)
        v = src[base : base + HS, :, lanes]
        col = lax.broadcasted_iota(jnp.int32, (HS, W, LANE), 1)
        for dj in range(7):
            d = dj - 3
            moved = v if d == 0 else pltpu.roll(v, (-d) % W, 1)
            sh[dj, base : base + HS, :, lanes] = jnp.where((col + d >= 0) & (col + d < S), moved, 0.0)
        acc = {r: total[r, :, lanes] if r in begun else start(r, lanes) for r in rows}
        for dj in range(7):
            ks = [k[6 - di, 6 - dj, :, lanes] if flip else k[di, dj, :, lanes] for di in range(7)]
            for i in range(base, base + HS):
                x = sh[dj, i, :, lanes]
                for r in rows:
                    if abs(r - i) <= 3:
                        acc[r] = acc[r] + ks[i - r + 3] * x
        for r in rows:
            total[r, :, lanes] = acc[r]

    loop(D // LANE, per_lanes)


def gelu_parts(x):
    t = 1.0 / (1.0 + 0.23164189 * jnp.abs(x))
    e = jnp.exp(-0.5 * (x * x))
    poly = t * (
        0.127414796
        + t * (-0.142248368 + t * (0.7107068705 + t * (-0.7265760135 + t * 0.5307027145)))
    )
    q = poly * e
    return jnp.where(x < 0.0, q, 1.0 - q), e


def convolve(take, x, sh, conv, k, kb):
    def bias(r, lanes):
        return jnp.broadcast_to(kb[:, lanes], (W, LANE))

    for half in range(2):
        take(half)
        conv_half(x, sh, k, conv, bias, half, False)


def mix(x, conv, gain, nb, w1, b1, w2, b2, ls, h, n, give, keep):
    for half in range(2):
        rows = slice(half * HR, half * HR + HR)
        c = conv[half * HS : half * HS + HS].reshape(HR, D)
        off = c - jnp.mean(c, axis=-1, keepdims=True)
        var = jnp.mean(off * off, axis=-1, keepdims=True)
        rstd = lax.rsqrt(var + norm_epsilon)
        hat = off * rstd
        n[rows, :] = (hat * gain[...] + nb[...]).astype(BF)
        if keep is not None:
            keep[0][rows, :] = hat
            keep[1][rows, :] = rstd
        for c in range(HID // CH):
            cols = slice(c * CH, c * CH + CH)
            a = dot(n[rows, :], w1[:, cols], 1, 0) + b1[:, cols]
            phi, e = gelu_parts(a)
            h[rows, cols] = (a * phi).astype(BF)
            if keep is not None:
                keep[2][rows, cols] = phi + a * e * 0.3989422804014327
        mixed = dot(h[rows, :], w2[...], 1, 0) + b2[...]
        if keep is not None:
            keep[3][rows, :] = mixed
        give(half, x[half * HS : half * HS + HS].reshape(HR, D) + ls[...] * mixed)


def unpadded(values):
    col = lax.broadcasted_iota(jnp.int32, values.shape, 1)
    return jnp.where(col < S, values, 0.0)


def to_section(src, dst, send, recv, section):
    return pltpu.make_async_remote_copy(
        src_ref=src,
        dst_ref=dst,
        send_sem=send,
        recv_sem=recv,
        device_id={"section": section},
        device_id_type=MESH,
    )


def greet_sections(barrier):
    s = lax.axis_index("section")
    count = lax.axis_size("section")
    for other in (lax.rem(s + 1, count), lax.rem(s + count - 1, count)):
        pl.semaphore_signal(barrier, inc=1, device_id={"section": other}, device_id_type=MESH)


def train_kernel(
    sources, marked,
    inputs, cot, probe, k, kb, gain, nb, w1, b1, w2, b2, ls,
    o_w1, o_w2, o_probe,
    w1f, w2f, w1b, w2b, x, sh, shd, conv, xhat, rstd, nrm, h, gp, mixed, dmb, du, dc, g,
    pt, gkb, ggain, gnb, gb1, gb2, gls, tiles, outgoing, incoming,
    fsend, frecv, bsend, brecv, f_s, f_r, b_s, b_r, w_in, w_out, e_s, e_r, block_of,
    o_k, o_kb, o_gain, o_nb, o_b1, o_b2, o_ls,
):
    s = lax.axis_index("section")
    last = lax.axis_size("section") - 1
    up = jnp.minimum(s + 1, last)
    down = jnp.maximum(s - 1, 0)
    me = lax.axis_index("member")

    loads = [
        pltpu.make_async_copy(w1, w1f, w_in.at[0]),
        pltpu.make_async_copy(w2, w2f, w_in.at[1]),
    ]
    for load in loads:
        load.start()
    barrier = pltpu.get_barrier_semaphore()
    greet_sections(barrier)
    for t in ORDER:
        pl.semaphore_signal(
            barrier, inc=1, device_id={"member": at_distance(me, t)}, device_id_type=MESH
        )
    for ref in (pt, gkb, ggain, gnb, gb1, gb2, gls):
        ref[...] = jnp.zeros_like(ref)
    pl.semaphore_wait(barrier, 2 + len(ORDER))

    def tables():
        def per_slot(t):
            to = at_distance(me, t)
            block = jnp.int32(0)
            for b in range(32):
                block = jnp.where((sources[b, to] == me) & (marked[b] == 1), b, block)
            block_of[t] = block

        loop(32, per_slot)

    @pl.when(s > 0)
    def _():
        tables()

    def take(half, first, given, arrived, wait, dst):
        rows = slice(half * HS, half * HS + HS)

        @pl.when(first)
        def _():
            dst[rows, S:W, :] = jnp.zeros((HS, W - S, D), F32)
            dst[rows, 0:S, :] = given[rows].astype(F32)

        @pl.when(jnp.logical_not(first))
        def _():
            wait()
            dst[rows] = arrived[rows].astype(F32)

    def half_copy(send, recv, sems, j, half, section):
        rows = pl.ds(half * HS, HS)
        return to_section(
            send.at[j, rows], recv.at[j, rows], sems[0].at[j, half], sems[1].at[j, half], section
        )

    def fwd_copy(j, half):
        return half_copy(fsend, frecv, (f_s, f_r), j, half, up)

    pieces = ((0, HS - 3), (HS - 3, HS), (HS, S))

    def bwd_copy(j, piece):
        rows = pl.ds(pieces[piece][0], pieces[piece][1] - pieces[piece][0])
        return to_section(
            bsend.at[j, rows], brecv.at[j, rows], b_s.at[j, piece], b_r.at[j, piece], down
        )

    def fwd(j):
        rows = pl.ds(pl.multiple_of(j * R, R), R)

        def before():
            @pl.when(j == 0)
            def _():
                for load in loads:
                    load.wait()

                def cast(i):
                    r = pl.ds(pl.multiple_of(i * 32, 32), 32)
                    w1b[r, :] = w1f[r, :].astype(BF)
                    r = pl.ds(pl.multiple_of(i * 128, 128), 128)
                    w2b[r, :] = w2f[r, :].astype(BF)

                loop(16, cast)

        def give(half, values):
            @pl.when(s < last)
            def _():
                fsend[j, half * HS : half * HS + HS] = unpadded(values.reshape(HS, W, D)).astype(BF)
                fwd_copy(j, half).start()

        convolve(
            lambda half: take(
                half, s == 0, inputs.at[j], frecv.at[j], fwd_copy(j, half).wait_recv, x.at[j]
            ),
            x.at[j], sh.at[j], conv, k, kb,
        )
        before()
        mix(
            x.at[j], conv, gain, nb, w1b, b1, w2b, b2, ls, h.at[rows, :], nrm.at[rows, :], give,
            (xhat.at[j], rstd.at[j], gp.at[j], mixed.at[j]),
        )

    loop(2, fwd)

    @pl.when(s == 0)
    def _():
        tables()

    def kernel_grad(j):
        def per_lanes(c):
            lanes = lanes_of(c)
            for dj in range(7):
                acc = [None] * 7
                for r in range(S):
                    d = dc[j, r, :, lanes]
                    for di in range(7):
                        if 0 <= r + di - 3 < S:
                            p = d * sh[j, dj, r + di - 3, :, lanes]
                            acc[di] = p if acc[di] is None else acc[di] + p
                for di in range(7):
                    pt[di, dj, :, lanes] += acc[di][0:8] + acc[di][8:16]

        loop(D // LANE, per_lanes)

    def bwd(j):
        def send_back(piece):
            part = slice(*pieces[piece])
            bsend[j, part] = unpadded(g[part] + conv[part]).astype(BF)
            bwd_copy(j, piece).start()

        def nothing(r, lanes):
            return jnp.zeros((W, LANE), F32)

        for half in range(2):
            base = pl.multiple_of(j * R, R)
            rows = slice(half * HR, half * HR + HR)
            both = half_rows(half, base)

            def arrive(half=half):
                for piece in ((0, 1), (2,))[half]:
                    bwd_copy(j, piece).wait_recv()

            take(half, s == last, cot.at[j], brecv.at[j], arrive, g)
            flat = g[half * HS : half * HS + HS].reshape(HR, D)
            dm = flat * ls[...]
            dmb[both, :] = dm.astype(BF)
            gb2[...] += jnp.sum(dm, axis=0, keepdims=True)
            gls[...] += jnp.sum(flat * mixed[j, rows, :], axis=0, keepdims=True)
            for c in range(HID // CH):
                cols = slice(c * CH, c * CH + CH)
                a = dot(dmb[both, :], w2b[cols, :], 1, 1) * gp[j, rows, cols]
                du[both, cols] = a.astype(BF)
                gb1[:, cols] += jnp.sum(a, axis=0, keepdims=True)
            dn = dot(du[both, :], w1b[...], 1, 1)
            hat = xhat[j, rows, :]
            dh = dn * gain[...]
            m1 = jnp.mean(dh, axis=-1, keepdims=True)
            m2 = jnp.mean(dh * hat, axis=-1, keepdims=True)
            d = rstd[j, rows, :] * (dh - m1 - hat * m2)
            dc[j, half * HS : half * HS + HS] = d.reshape(HS, W, D)
            ggain[...] += jnp.sum(dn * hat, axis=0, keepdims=True)
            gnb[...] += jnp.sum(dn, axis=0, keepdims=True)
            gkb[...] += jnp.sum(d, axis=0, keepdims=True)

            @pl.when(s > 0)
            def _(half=half):
                conv_half(dc.at[j], shd, k, conv, nothing, half, True)
                for piece in ((0,), (1, 2))[half]:
                    send_back(piece)

    loop(2, bwd)

    for c in range(4):
        cols = pl.ds(c * 512, 512)
        new = w1f[:, cols] - learning_rate * dot(nrm[...], du[:, cols], 0, 0)
        w1f[:, cols] = new
        for q in range(4):
            tiles[4 * c + q] = new[:, q * TILE : (q + 1) * TILE].astype(BF)
    for r in range(HID // D):
        rows = pl.ds(r * D, D)
        new = w2f[rows, :] - learning_rate * dot(h[:, rows], dmb[...], 0, 0)
        w2f[rows, :] = new
        for q in range(4):
            tiles[16 + 4 * q + r] = new[:, q * TILE : (q + 1) * TILE].astype(BF)

    def push_copy(t):
        return pltpu.make_async_remote_copy(
            src_ref=outgoing.at[t],
            dst_ref=incoming.at[t],
            send_sem=e_s.at[t],
            recv_sem=e_r.at[t],
            device_id={"member": at_distance(me, t)},
            device_id_type=MESH,
        )

    for t in ORDER:
        outgoing[t] = tiles[block_of[t]]
        push_copy(t).start()

    loop(2, kernel_grad)
    for di in range(7):
        for dj in range(7):
            o_k[di, dj] = k[di, dj] - learning_rate * jnp.sum(pt[di, dj], axis=0, keepdims=True)
    for old, grad, new in (
        (kb, gkb, o_kb), (gain, ggain, o_gain), (nb, gnb, o_nb),
        (b1, gb1, o_b1), (b2, gb2, o_b2), (ls, gls, o_ls),
    ):
        new[...] = old[...] - learning_rate * grad[...]

    def probe_take(half):
        take(half, s == 0, probe, frecv.at[2], fwd_copy(2, half).wait_recv, x.at[0])

    def probe_give(half, values):
        rows = slice(half * HS, half * HS + HS)
        fsend[2, rows] = unpadded(values.reshape(HS, W, D)).astype(BF)

        @pl.when(s < last)
        def _():
            fwd_copy(2, half).start()

        o_probe[rows] = fsend[2, rows, 0:S, :]

    @pl.when(s == 0)
    def _():
        convolve(probe_take, x.at[0], shd, conv, o_k, o_kb)

    for t in ORDER:
        push_copy(t).wait_recv()

    def slot_of(b):
        source = sources[b, me]
        z = lax.rem(me // 8 - source // 8 + 4, 4)
        x = lax.rem(lax.rem(me // 2, 4) - lax.rem(source // 2, 4) + 4, 4)
        c = lax.rem(lax.rem(me, 2) + lax.rem(source, 2), 2)
        return z * 8 + x * 2 + c

    def place_in(b):
        w1b[:, lanes_of(b)] = jnp.where(marked[b] == 1, incoming[slot_of(b)], tiles[b])

    loop(16, place_in)

    def place_out(r):
        for c in range(4):
            b = 16 + 4 * c + r
            w2b[pl.ds(pl.multiple_of(r * D, D), D), pl.ds(c * TILE, TILE)] = jnp.where(
                marked[b] == 1, incoming[slot_of(b)], tiles[b]
            )

    loop(4, place_out)

    stores = [
        pltpu.make_async_copy(w1f, o_w1, w_out.at[0]),
        pltpu.make_async_copy(w2f, o_w2, w_out.at[1]),
    ]

    def finish():
        def finish_in(b):
            lanes = lanes_of(b)
            w1f[:, lanes] = jnp.where(marked[b] == 1, w1b[:, lanes].astype(F32), w1f[:, lanes])

        def finish_out(r):
            rows = pl.ds(pl.multiple_of(r * D, D), D)
            for c in range(4):
                cols = pl.ds(c * TILE, TILE)
                w2f[rows, cols] = jnp.where(
                    marked[16 + 4 * c + r] == 1, w2b[rows, cols].astype(F32), w2f[rows, cols]
                )

        loop(16, finish_in)
        stores[0].start()
        loop(4, finish_out)
        stores[1].start()

    @pl.when(s > 0)
    def _():
        finish()
        convolve(probe_take, x.at[0], shd, conv, o_k, o_kb)

    mix(
        x.at[0], conv, o_gain, o_nb, w1b, o_b1, w2b, o_b2, o_ls,
        h.at[pl.ds(0, R), :], nrm.at[pl.ds(0, R), :], probe_give, None,
    )

    @pl.when(s == 0)
    def _():
        finish()

    for copy in stores:
        copy.wait()
    for t in ORDER:
        push_copy(t).wait_send()
    for half in range(2):
        for j in range(3):

            @pl.when(s < last)
            def _(j=j, half=half):
                fwd_copy(j, half).wait_send()

    for piece in range(3):
        for j in range(2):

            @pl.when(s > 0)
            def _(j=j, piece=piece):
                bwd_copy(j, piece).wait_send()


def vmem(n):
    return [pl.BlockSpec(memory_space=pltpu.VMEM)] * n


def hbm(n):
    return [pl.BlockSpec(memory_space=pltpu.HBM)] * n


def params(collective, mib):
    return pltpu.CompilerParams(
        collective_id=collective, has_side_effects=True, vmem_limit_bytes=mib * 2**20
    )


def train(tables, inputs, cot, probe, small, w1, w2):
    k, kb, gain, nb, b1, b2, ls = small
    dma = pltpu.SemaphoreType.DMA
    V = pltpu.VMEM
    shape = jax.ShapeDtypeStruct
    wide = (2, S, W, D)
    return pl.pallas_call(
        train_kernel,
        out_shape=(shape((D, HID), F32), shape((HID, D), F32), shape((S, S, D), BF)),
        in_specs=[pl.BlockSpec(memory_space=pltpu.SMEM)] * 2 + vmem(7) + hbm(1) + vmem(1) + hbm(1) + vmem(2),
        out_specs=hbm(2) + vmem(1),
        scratch_shapes=[
            V((D, HID), F32), V((HID, D), F32), V((D, HID), BF), V((HID, D), BF),
            V(wide, F32), V((2, 7, S, W, D), F32), V((7, S, W, D), F32), V((S, W, D), F32),
            V((2, R, D), F32), V((2, R, 1), F32), V((2 * R, D), BF), V((2 * R, HID), BF),
            V((2, R, HID), F32), V((2, R, D), F32), V((2 * R, D), BF), V((2 * R, HID), BF),
            V(wide, F32), V((S, W, D), F32),
            V((7, 7, 8, D), F32), V((1, D), F32), V((1, D), F32), V((1, D), F32),
            V((1, HID), F32), V((1, D), F32), V((1, D), F32),
            V((32, D, TILE), BF), V((32, D, TILE), BF), V((32, D, TILE), BF),
            V((3, S, W, D), BF), V((3, S, W, D), BF), V(wide, BF), V(wide, BF),
            dma((3, 2)), dma((3, 2)), dma((2, 3)), dma((2, 3)), dma((2,)), dma((2,)),
            dma((32,)), dma((32,)), pltpu.SMEM((32,), jnp.int32),
            V((7, 7, 1, D), F32), V((1, D), F32), V((1, D), F32), V((1, D), F32),
            V((1, HID), F32), V((1, D), F32), V((1, D), F32),
        ],
        compiler_params=params(0, 60),
        name="train",
    )(*tables, inputs, cot, probe, k, kb, gain, nb, w1, b1, w2, b2, ls)


def local(
    inputs, cotangent, probe, dw_kernel, dw_bias, norm_gain, norm_bias, w_in, b_in, w_out, b_out,
    layer_scale, shuffle_mask, source_member,
):
    small = (
        dw_kernel[0, 0][:, :, None, :], dw_bias[0], norm_gain[0], norm_bias[0], b_in[0], b_out[0],
        layer_scale[0],
    )
    marked = shuffle_mask[0]
    new_in, new_out, out = train(
        (source_member[0], marked), inputs[0, :, 0], cotangent[0, :, 0], probe[0, 0], small,
        w_in[0, 0], w_out[0, 0],
    )
    return new_in[None, None], new_out[None, None], out[None, None, None]


def solution(mesh):
    return jax.shard_map(
        local,
        mesh=mesh,
        in_specs=(
            P("member", None, None, None, None, None),
            P("member", None, None, None, None, None),
            P("member", None, None, None, None),
            P("member", "section", None, None, None),
            P("member", "section", None),
            P("member", "section", None),
            P("member", "section", None),
            P("member", "section", None, None),
            P("member", "section", None),
            P("member", "section", None, None),
            P("member", "section", None),
            P("member", "section", None),
            P("section", None),
            P("section", None, None),
        ),
        out_specs=(
            P("member", "section", None, None),
            P("member", "section", None, None),
            P("member", "section", None, None, None, None),
        ),
        check_vma=False,
    )
```

```python
import jax
import jax.numpy as jnp
from jax import lax
from jax.experimental import pallas as pl
from jax.experimental.pallas import tpu as pltpu
from jax.sharding import PartitionSpec as P

MESH = pl.DeviceIdType.MESH
BF = jnp.bfloat16
F32 = jnp.float32
S = 14
W = 16
R = S * W
HS, HR = S // 2, R // 2
D = 512
HID = 2048
LANE = 128
TILE = 128
CH = 256
learning_rate = 0.001
norm_epsilon = 1e-06

CHIPS = (
    (0, 0), (0, 1), (1, 0), (0, 3), (3, 0), (1, 1), (3, 3), (1, 3), (3, 1),
    (0, 2), (2, 0), (2, 2), (1, 2), (2, 1), (3, 2), (2, 3),
)
ORDER = tuple(z * 8 + x * 2 + c for c in (1, 0) for z, x in CHIPS if (z, x, c) != (0, 0, 0))

RELAYED = tuple(z * 8 + x * 2 + c for z, x, c in ((2, 2, 0), (2, 2, 1), (1, 2, 1), (2, 1, 1)))
EARLY = 14
DIRECT = tuple(t for t in ORDER if t not in RELAYED)
SEQUENCE = tuple(
    t for i, r in enumerate(RELAYED) for t in (DIRECT[2 * i], r, DIRECT[2 * i + 1])
) + DIRECT[2 * len(RELAYED) :]


def at_distance(me, t, sign=1):
    z = lax.rem(me // 8 + sign * (t // 8) + 4, 4)
    x = lax.rem(lax.rem(me // 2, 4) + sign * (t // 2 % 4) + 4, 4)
    c = lax.rem(lax.rem(me, 2) + t % 2, 2)
    return z * 8 + x * 2 + c


def dot(a, b, ca, cb):
    return lax.dot_general(a, b, (((ca,), (cb,)), ((), ())), preferred_element_type=F32)


def loop(n, body):
    lax.fori_loop(0, n, lambda i, c: (body(i), c)[1], 0)


def lanes_of(c):
    return pl.ds(pl.multiple_of(c * LANE, LANE), LANE)


def half_rows(half, base=0):
    return pl.ds(pl.multiple_of(base + half * HR, HR), HR)


def conv_half(src, sh, k, total, start, half, flip):
    base = half * HS
    rows = range(0, HS + 3) if half == 0 else range(HS - 3, S)
    begun = () if half == 0 else range(HS - 3, HS + 3)

    def per_lanes(c):
        lanes = lanes_of(c)
        v = src[base : base + HS, :, lanes]
        col = lax.broadcasted_iota(jnp.int32, (HS, W, LANE), 1)
        for dj in range(7):
            d = dj - 3
            moved = v if d == 0 else pltpu.roll(v, (-d) % W, 1)
            sh[dj, base : base + HS, :, lanes] = jnp.where((col + d >= 0) & (col + d < S), moved, 0.0)
        acc = {r: total[r, :, lanes] if r in begun else start(r, lanes) for r in rows}
        for dj in range(7):
            ks = [k[6 - di, 6 - dj, :, lanes] if flip else k[di, dj, :, lanes] for di in range(7)]
            for i in range(base, base + HS):
                x = sh[dj, i, :, lanes]
                for r in rows:
                    if abs(r - i) <= 3:
                        acc[r] = acc[r] + ks[i - r + 3] * x
        for r in rows:
            total[r, :, lanes] = acc[r]

    loop(D // LANE, per_lanes)


def gelu_parts(x):
    t = 1.0 / (1.0 + 0.23164189 * jnp.abs(x))
    e = jnp.exp(-0.5 * (x * x))
    poly = t * (
        0.127414796
        + t * (-0.142248368 + t * (0.7107068705 + t * (-0.7265760135 + t * 0.5307027145)))
    )
    q = poly * e
    return jnp.where(x < 0.0, q, 1.0 - q), e


def convolve(take, x, sh, conv, k, kb):
    def bias(r, lanes):
        return jnp.broadcast_to(kb[:, lanes], (W, LANE))

    for half in range(2):
        take(half)
        conv_half(x, sh, k, conv, bias, half, False)


def mix(x, conv, gain, nb, w1, b1, w2, b2, ls, h, n, give, keep):
    for half in range(2):
        rows = slice(half * HR, half * HR + HR)
        c = conv[half * HS : half * HS + HS].reshape(HR, D)
        off = c - jnp.mean(c, axis=-1, keepdims=True)
        var = jnp.mean(off * off, axis=-1, keepdims=True)
        rstd = lax.rsqrt(var + norm_epsilon)
        hat = off * rstd
        n[rows, :] = (hat * gain[...] + nb[...]).astype(BF)
        if keep is not None:
            keep[0][rows, :] = hat
            keep[1][rows, :] = rstd
        for c in range(HID // CH):
            cols = slice(c * CH, c * CH + CH)
            a = dot(n[rows, :], w1[:, cols], 1, 0) + b1[:, cols]
            phi, e = gelu_parts(a)
            h[rows, cols] = (a * phi).astype(BF)
            if keep is not None:
                keep[2][rows, cols] = phi + a * e * 0.3989422804014327
        mixed = dot(h[rows, :], w2[...], 1, 0) + b2[...]
        if keep is not None:
            keep[3][rows, :] = mixed
        give(half, x[half * HS : half * HS + HS].reshape(HR, D) + ls[...] * mixed)


def unpadded(values):
    col = lax.broadcasted_iota(jnp.int32, values.shape, 1)
    return jnp.where(col < S, values, 0.0)


def to_section(src, dst, send, recv, section):
    return pltpu.make_async_remote_copy(
        src_ref=src,
        dst_ref=dst,
        send_sem=send,
        recv_sem=recv,
        device_id={"section": section},
        device_id_type=MESH,
    )


def greet_sections(barrier):
    s = lax.axis_index("section")
    count = lax.axis_size("section")
    for other in (lax.rem(s + 1, count), lax.rem(s + count - 1, count)):
        pl.semaphore_signal(barrier, inc=1, device_id={"section": other}, device_id_type=MESH)


def train_kernel(
    sources, marked,
    inputs, cot, probe, k, kb, gain, nb, w1, b1, w2, b2, ls,
    o_w1, o_w2, o_probe,
    w1f, w2f, w1b, w2b, x, sh, shd, conv, xhat, rstd, nrm, h, gp, mixed, dmb, du, dc, g,
    pt, gkb, ggain, gnb, gb1, gb2, gls, tiles, outgoing, incoming,
    fsend, frecv, bsend, brecv, f_s, f_r, b_s, b_r, w_in, w_out, e_s, e_r, block_of, relay, r_s, r_r,
    o_k, o_kb, o_gain, o_nb, o_b1, o_b2, o_ls,
):
    s = lax.axis_index("section")
    last = lax.axis_size("section") - 1
    up = jnp.minimum(s + 1, last)
    down = jnp.maximum(s - 1, 0)
    me = lax.axis_index("member")

    loads = [
        pltpu.make_async_copy(w1, w1f, w_in.at[0]),
        pltpu.make_async_copy(w2, w2f, w_in.at[1]),
    ]
    for load in loads:
        load.start()
    barrier = pltpu.get_barrier_semaphore()
    greet_sections(barrier)
    for t in ORDER:
        pl.semaphore_signal(
            barrier, inc=1, device_id={"member": at_distance(me, t)}, device_id_type=MESH
        )
    for ref in (pt, gkb, ggain, gnb, gb1, gb2, gls):
        ref[...] = jnp.zeros_like(ref)
    pl.semaphore_wait(barrier, 2 + len(ORDER))

    def tables():
        def per_slot(t):
            to = at_distance(me, t)
            block = jnp.int32(0)
            for b in range(32):
                block = jnp.where((sources[b, to] == me) & (marked[b] == 1), b, block)
            block_of[t] = block

        loop(32, per_slot)

    @pl.when(s > 0)
    def _():
        tables()

    def take(half, first, given, arrived, wait, dst):
        rows = slice(half * HS, half * HS + HS)

        @pl.when(first)
        def _():
            dst[rows, S:W, :] = jnp.zeros((HS, W - S, D), F32)
            dst[rows, 0:S, :] = given[rows].astype(F32)

        @pl.when(jnp.logical_not(first))
        def _():
            wait()
            dst[rows] = arrived[rows].astype(F32)

    def half_copy(send, recv, sems, j, half, section):
        rows = pl.ds(half * HS, HS)
        return to_section(
            send.at[j, rows], recv.at[j, rows], sems[0].at[j, half], sems[1].at[j, half], section
        )

    def fwd_copy(j, half):
        return half_copy(fsend, frecv, (f_s, f_r), j, half, up)

    pieces = ((0, HS - 3), (HS - 3, HS), (HS, S))

    def bwd_copy(j, piece):
        rows = pl.ds(pieces[piece][0], pieces[piece][1] - pieces[piece][0])
        return to_section(
            bsend.at[j, rows], brecv.at[j, rows], b_s.at[j, piece], b_r.at[j, piece], down
        )

    def fwd(j):
        rows = pl.ds(pl.multiple_of(j * R, R), R)

        def before():
            @pl.when(j == 0)
            def _():
                for load in loads:
                    load.wait()

                def cast(i):
                    r = pl.ds(pl.multiple_of(i * 32, 32), 32)
                    w1b[r, :] = w1f[r, :].astype(BF)
                    r = pl.ds(pl.multiple_of(i * 128, 128), 128)
                    w2b[r, :] = w2f[r, :].astype(BF)

                loop(16, cast)

        def give(half, values):
            @pl.when(s < last)
            def _():
                fsend[j, half * HS : half * HS + HS] = unpadded(values.reshape(HS, W, D)).astype(BF)
                fwd_copy(j, half).start()

        convolve(
            lambda half: take(
                half, s == 0, inputs.at[j], frecv.at[j], fwd_copy(j, half).wait_recv, x.at[j]
            ),
            x.at[j], sh.at[j], conv, k, kb,
        )
        before()
        mix(
            x.at[j], conv, gain, nb, w1b, b1, w2b, b2, ls, h.at[rows, :], nrm.at[rows, :], give,
            (xhat.at[j], rstd.at[j], gp.at[j], mixed.at[j]),
        )

    loop(2, fwd)

    @pl.when(s == 0)
    def _():
        tables()

    def kernel_grad(j):
        def per_lanes(c):
            lanes = lanes_of(c)
            for dj in range(7):
                acc = [None] * 7
                for r in range(S):
                    d = dc[j, r, :, lanes]
                    for di in range(7):
                        if 0 <= r + di - 3 < S:
                            p = d * sh[j, dj, r + di - 3, :, lanes]
                            acc[di] = p if acc[di] is None else acc[di] + p
                for di in range(7):
                    pt[di, dj, :, lanes] += acc[di][0:8] + acc[di][8:16]

        loop(D // LANE, per_lanes)

    def bwd(j):
        def send_back(piece):
            part = slice(*pieces[piece])
            bsend[j, part] = unpadded(g[part] + conv[part]).astype(BF)
            bwd_copy(j, piece).start()

        def nothing(r, lanes):
            return jnp.zeros((W, LANE), F32)

        for half in range(2):
            base = pl.multiple_of(j * R, R)
            rows = slice(half * HR, half * HR + HR)
            both = half_rows(half, base)

            def arrive(half=half):
                for piece in ((0, 1), (2,))[half]:
                    bwd_copy(j, piece).wait_recv()

            take(half, s == last, cot.at[j], brecv.at[j], arrive, g)
            flat = g[half * HS : half * HS + HS].reshape(HR, D)
            dm = flat * ls[...]
            dmb[both, :] = dm.astype(BF)
            gb2[...] += jnp.sum(dm, axis=0, keepdims=True)
            gls[...] += jnp.sum(flat * mixed[j, rows, :], axis=0, keepdims=True)
            for c in range(HID // CH):
                cols = slice(c * CH, c * CH + CH)
                a = dot(dmb[both, :], w2b[cols, :], 1, 1) * gp[j, rows, cols]
                du[both, cols] = a.astype(BF)
                gb1[:, cols] += jnp.sum(a, axis=0, keepdims=True)
            dn = dot(du[both, :], w1b[...], 1, 1)
            hat = xhat[j, rows, :]
            dh = dn * gain[...]
            m1 = jnp.mean(dh, axis=-1, keepdims=True)
            m2 = jnp.mean(dh * hat, axis=-1, keepdims=True)
            d = rstd[j, rows, :] * (dh - m1 - hat * m2)
            dc[j, half * HS : half * HS + HS] = d.reshape(HS, W, D)
            ggain[...] += jnp.sum(dn * hat, axis=0, keepdims=True)
            gnb[...] += jnp.sum(dn, axis=0, keepdims=True)
            gkb[...] += jnp.sum(d, axis=0, keepdims=True)

            @pl.when(s > 0)
            def _(half=half):
                conv_half(dc.at[j], shd, k, conv, nothing, half, True)
                for piece in ((0,), (1, 2))[half]:
                    send_back(piece)

    loop(2, bwd)

    for c in range(4):
        cols = pl.ds(c * 512, 512)
        new = w1f[:, cols] - learning_rate * dot(nrm[...], du[:, cols], 0, 0)
        w1f[:, cols] = new
        for q in range(4):
            tiles[4 * c + q] = new[:, q * TILE : (q + 1) * TILE].astype(BF)
    for r in range(HID // D):
        rows = pl.ds(r * D, D)
        new = w2f[rows, :] - learning_rate * dot(h[:, rows], dmb[...], 0, 0)
        w2f[rows, :] = new
        for q in range(4):
            tiles[16 + 4 * q + r] = new[:, q * TILE : (q + 1) * TILE].astype(BF)

    def push_copy(t):
        return pltpu.make_async_remote_copy(
            src_ref=outgoing.at[t],
            dst_ref=incoming.at[t],
            send_sem=e_s.at[t],
            recv_sem=e_r.at[t],
            device_id={"member": at_distance(me, t)},
            device_id_type=MESH,
        )

    partner = last - s

    def relay_copy(i):
        return to_section(
            outgoing.at[RELAYED[i]], relay.at[0, i], e_s.at[RELAYED[i]], r_r.at[0, i], partner
        )

    def relay_across(i):
        return pltpu.make_async_remote_copy(
            src_ref=relay.at[0, i],
            dst_ref=relay.at[1, i],
            send_sem=r_s.at[0, i],
            recv_sem=r_r.at[1, i],
            device_id={"member": at_distance(me, RELAYED[i])},
            device_id_type=MESH,
        )

    def relay_back(i):
        return to_section(
            relay.at[1, i], incoming.at[RELAYED[i]], r_s.at[1, i], e_r.at[RELAYED[i]], partner
        )

    def push(t):
        outgoing[t] = tiles[block_of[t]]
        if t in RELAYED:

            @pl.when(s == 0)
            def _():
                relay_copy(RELAYED.index(t)).start()

            @pl.when(s > 0)
            def _():
                push_copy(t).start()
        else:
            push_copy(t).start()

    for t in SEQUENCE[:EARLY]:
        push(t)

    later = list(SEQUENCE[EARLY:])
    for i in range(len(RELAYED) + 1):
        if i < len(RELAYED):

            @pl.when(s == last)
            def _(i=i):
                relay_copy(i).wait_recv()
                relay_across(i).start()

        if i > 0:

            @pl.when(s == last)
            def _(i=i - 1):
                relay_across(i).wait_recv()
                relay_back(i).start()

        push(later.pop(0))
    for t in later:
        push(t)

    loop(2, kernel_grad)
    for di in range(7):
        for dj in range(7):
            o_k[di, dj] = k[di, dj] - learning_rate * jnp.sum(pt[di, dj], axis=0, keepdims=True)
    for old, grad, new in (
        (kb, gkb, o_kb), (gain, ggain, o_gain), (nb, gnb, o_nb),
        (b1, gb1, o_b1), (b2, gb2, o_b2), (ls, gls, o_ls),
    ):
        new[...] = old[...] - learning_rate * grad[...]

    def probe_take(half):
        take(half, s == 0, probe, frecv.at[2], fwd_copy(2, half).wait_recv, x.at[0])

    def probe_give(half, values):
        rows = slice(half * HS, half * HS + HS)
        fsend[2, rows] = unpadded(values.reshape(HS, W, D)).astype(BF)

        @pl.when(s < last)
        def _():
            fwd_copy(2, half).start()

        o_probe[rows] = fsend[2, rows, 0:S, :]

    @pl.when(s == 0)
    def _():
        convolve(probe_take, x.at[0], shd, conv, o_k, o_kb)

    for t in ORDER:
        push_copy(t).wait_recv()

    def slot_of(b):
        source = sources[b, me]
        z = lax.rem(me // 8 - source // 8 + 4, 4)
        x = lax.rem(lax.rem(me // 2, 4) - lax.rem(source // 2, 4) + 4, 4)
        c = lax.rem(lax.rem(me, 2) + lax.rem(source, 2), 2)
        return z * 8 + x * 2 + c

    def place_in(b):
        w1b[:, lanes_of(b)] = jnp.where(marked[b] == 1, incoming[slot_of(b)], tiles[b])

    loop(16, place_in)

    def place_out(r):
        for c in range(4):
            b = 16 + 4 * c + r
            w2b[pl.ds(pl.multiple_of(r * D, D), D), pl.ds(c * TILE, TILE)] = jnp.where(
                marked[b] == 1, incoming[slot_of(b)], tiles[b]
            )

    loop(4, place_out)

    stores = [
        pltpu.make_async_copy(w1f, o_w1, w_out.at[0]),
        pltpu.make_async_copy(w2f, o_w2, w_out.at[1]),
    ]

    def finish():
        def finish_in(b):
            lanes = lanes_of(b)
            w1f[:, lanes] = jnp.where(marked[b] == 1, w1b[:, lanes].astype(F32), w1f[:, lanes])

        def finish_out(r):
            rows = pl.ds(pl.multiple_of(r * D, D), D)
            for c in range(4):
                cols = pl.ds(c * TILE, TILE)
                w2f[rows, cols] = jnp.where(
                    marked[16 + 4 * c + r] == 1, w2b[rows, cols].astype(F32), w2f[rows, cols]
                )

        loop(16, finish_in)
        stores[0].start()
        loop(4, finish_out)
        stores[1].start()

    @pl.when(s > 0)
    def _():
        finish()
        convolve(probe_take, x.at[0], shd, conv, o_k, o_kb)

    mix(
        x.at[0], conv, o_gain, o_nb, w1b, o_b1, w2b, o_b2, o_ls,
        h.at[pl.ds(0, R), :], nrm.at[pl.ds(0, R), :], probe_give, None,
    )

    @pl.when(s == 0)
    def _():
        finish()

    for copy in stores:
        copy.wait()
    for t in ORDER:
        push_copy(t).wait_send()

    @pl.when(s == last)
    def _():
        for i in range(len(RELAYED)):
            relay_across(i).wait_send()
            relay_back(i).wait_send()

    for half in range(2):
        for j in range(3):

            @pl.when(s < last)
            def _(j=j, half=half):
                fwd_copy(j, half).wait_send()

    for piece in range(3):
        for j in range(2):

            @pl.when(s > 0)
            def _(j=j, piece=piece):
                bwd_copy(j, piece).wait_send()


def vmem(n):
    return [pl.BlockSpec(memory_space=pltpu.VMEM)] * n


def hbm(n):
    return [pl.BlockSpec(memory_space=pltpu.HBM)] * n


def params(collective, mib):
    return pltpu.CompilerParams(
        collective_id=collective, has_side_effects=True, vmem_limit_bytes=mib * 2**20
    )


def train(tables, inputs, cot, probe, small, w1, w2):
    k, kb, gain, nb, b1, b2, ls = small
    dma = pltpu.SemaphoreType.DMA
    V = pltpu.VMEM
    shape = jax.ShapeDtypeStruct
    wide = (2, S, W, D)
    return pl.pallas_call(
        train_kernel,
        out_shape=(shape((D, HID), F32), shape((HID, D), F32), shape((S, S, D), BF)),
        in_specs=[pl.BlockSpec(memory_space=pltpu.SMEM)] * 2 + vmem(7) + hbm(1) + vmem(1) + hbm(1) + vmem(2),
        out_specs=hbm(2) + vmem(1),
        scratch_shapes=[
            V((D, HID), F32), V((HID, D), F32), V((D, HID), BF), V((HID, D), BF),
            V(wide, F32), V((2, 7, S, W, D), F32), V((7, S, W, D), F32), V((S, W, D), F32),
            V((2, R, D), F32), V((2, R, 1), F32), V((2 * R, D), BF), V((2 * R, HID), BF),
            V((2, R, HID), F32), V((2, R, D), F32), V((2 * R, D), BF), V((2 * R, HID), BF),
            V(wide, F32), V((S, W, D), F32),
            V((7, 7, 8, D), F32), V((1, D), F32), V((1, D), F32), V((1, D), F32),
            V((1, HID), F32), V((1, D), F32), V((1, D), F32),
            V((32, D, TILE), BF), V((32, D, TILE), BF), V((32, D, TILE), BF),
            V((3, S, W, D), BF), V((3, S, W, D), BF), V(wide, BF), V(wide, BF),
            dma((3, 2)), dma((3, 2)), dma((2, 3)), dma((2, 3)), dma((2,)), dma((2,)),
            dma((32,)), dma((32,)), pltpu.SMEM((32,), jnp.int32),
            V((2, len(RELAYED), D, TILE), BF), dma((2, len(RELAYED))), dma((2, len(RELAYED))),
            V((7, 7, 1, D), F32), V((1, D), F32), V((1, D), F32), V((1, D), F32),
            V((1, HID), F32), V((1, D), F32), V((1, D), F32),
        ],
        compiler_params=params(0, 60),
        name="train",
    )(*tables, inputs, cot, probe, k, kb, gain, nb, w1, b1, w2, b2, ls)


def local(
    inputs, cotangent, probe, dw_kernel, dw_bias, norm_gain, norm_bias, w_in, b_in, w_out, b_out,
    layer_scale, shuffle_mask, source_member,
):
    small = (
        dw_kernel[0, 0][:, :, None, :], dw_bias[0], norm_gain[0], norm_bias[0], b_in[0], b_out[0],
        layer_scale[0],
    )
    marked = shuffle_mask[0]
    new_in, new_out, out = train(
        (source_member[0], marked), inputs[0, :, 0], cotangent[0, :, 0], probe[0, 0], small,
        w_in[0, 0], w_out[0, 0],
    )
    return new_in[None, None], new_out[None, None], out[None, None, None]


def solution(mesh):
    return jax.shard_map(
        local,
        mesh=mesh,
        in_specs=(
            P("member", None, None, None, None, None),
            P("member", None, None, None, None, None),
            P("member", None, None, None, None),
            P("member", "section", None, None, None),
            P("member", "section", None),
            P("member", "section", None),
            P("member", "section", None),
            P("member", "section", None, None),
            P("member", "section", None),
            P("member", "section", None, None),
            P("member", "section", None),
            P("member", "section", None),
            P("section", None),
            P("section", None, None),
        ),
        out_specs=(
            P("member", "section", None, None),
            P("member", "section", None, None),
            P("member", "section", None, None, None, None),
        ),
        check_vma=False,
    )
```

```python
import jax
import jax.numpy as jnp
from jax import lax
from jax.experimental import pallas as pl
from jax.experimental.pallas import tpu as pltpu
from jax.sharding import PartitionSpec as P

MESH = pl.DeviceIdType.MESH
BF = jnp.bfloat16
F32 = jnp.float32
S = 14
W = 16
R = S * W
HS, HR = S // 2, R // 2
D = 512
HID = 2048
LANE = 128
TILE = 128
CH = 256
learning_rate = 0.001
norm_epsilon = 1e-06

CHIPS = (
    (0, 0), (0, 1), (1, 0), (0, 3), (3, 0), (1, 1), (3, 3), (1, 3), (3, 1),
    (0, 2), (2, 0), (2, 2), (1, 2), (2, 1), (3, 2), (2, 3),
)
ORDER = tuple(z * 8 + x * 2 + c for c in (1, 0) for z, x in CHIPS if (z, x, c) != (0, 0, 0))

RELAYED = tuple(
    z * 8 + x * 2 + c for z, x, c in ((2, 2, 0), (2, 2, 1), (1, 2, 1), (2, 1, 1), (3, 2, 1))
)
EARLY = 14
BOTH = 0
DIRECT = tuple(t for t in ORDER if t not in RELAYED)
SEQUENCE = tuple(
    t for i, r in enumerate(RELAYED) for t in (DIRECT[2 * i], r, DIRECT[2 * i + 1])
) + DIRECT[2 * len(RELAYED) :]


def at_distance(me, t, sign=1):
    z = lax.rem(me // 8 + sign * (t // 8) + 4, 4)
    x = lax.rem(lax.rem(me // 2, 4) + sign * (t // 2 % 4) + 4, 4)
    c = lax.rem(lax.rem(me, 2) + t % 2, 2)
    return z * 8 + x * 2 + c


def dot(a, b, ca, cb):
    return lax.dot_general(a, b, (((ca,), (cb,)), ((), ())), preferred_element_type=F32)


def loop(n, body):
    lax.fori_loop(0, n, lambda i, c: (body(i), c)[1], 0)


def lanes_of(c):
    return pl.ds(pl.multiple_of(c * LANE, LANE), LANE)


def half_rows(half, base=0):
    return pl.ds(pl.multiple_of(base + half * HR, HR), HR)


def conv_half(src, sh, k, total, start, half, flip):
    base = half * HS
    rows = range(0, HS + 3) if half == 0 else range(HS - 3, S)
    begun = () if half == 0 else range(HS - 3, HS + 3)

    def per_lanes(c):
        lanes = lanes_of(c)
        v = src[base : base + HS, :, lanes]
        col = lax.broadcasted_iota(jnp.int32, (HS, W, LANE), 1)
        for dj in range(7):
            d = dj - 3
            moved = v if d == 0 else pltpu.roll(v, (-d) % W, 1)
            sh[dj, base : base + HS, :, lanes] = jnp.where((col + d >= 0) & (col + d < S), moved, 0.0)
        acc = {r: total[r, :, lanes] if r in begun else start(r, lanes) for r in rows}
        for dj in range(7):
            ks = [k[6 - di, 6 - dj, :, lanes] if flip else k[di, dj, :, lanes] for di in range(7)]
            for i in range(base, base + HS):
                x = sh[dj, i, :, lanes]
                for r in rows:
                    if abs(r - i) <= 3:
                        acc[r] = acc[r] + ks[i - r + 3] * x
        for r in rows:
            total[r, :, lanes] = acc[r]

    loop(D // LANE, per_lanes)


def gelu_parts(x):
    t = 1.0 / (1.0 + 0.23164189 * jnp.abs(x))
    e = jnp.exp(-0.5 * (x * x))
    poly = t * (
        0.127414796
        + t * (-0.142248368 + t * (0.7107068705 + t * (-0.7265760135 + t * 0.5307027145)))
    )
    q = poly * e
    return jnp.where(x < 0.0, q, 1.0 - q), e


def convolve(take, x, sh, conv, k, kb):
    def bias(r, lanes):
        return jnp.broadcast_to(kb[:, lanes], (W, LANE))

    for half in range(2):
        take(half)
        conv_half(x, sh, k, conv, bias, half, False)


def mix(x, conv, gain, nb, w1, b1, w2, b2, ls, h, n, give, keep):
    for half in range(2):
        rows = slice(half * HR, half * HR + HR)
        c = conv[half * HS : half * HS + HS].reshape(HR, D)
        off = c - jnp.mean(c, axis=-1, keepdims=True)
        var = jnp.mean(off * off, axis=-1, keepdims=True)
        rstd = lax.rsqrt(var + norm_epsilon)
        hat = off * rstd
        n[rows, :] = (hat * gain[...] + nb[...]).astype(BF)
        if keep is not None:
            keep[0][rows, :] = hat
            keep[1][rows, :] = rstd
        for c in range(HID // CH):
            cols = slice(c * CH, c * CH + CH)
            a = dot(n[rows, :], w1[:, cols], 1, 0) + b1[:, cols]
            phi, e = gelu_parts(a)
            h[rows, cols] = (a * phi).astype(BF)
            if keep is not None:
                keep[2][rows, cols] = phi + a * e * 0.3989422804014327
        mixed = dot(h[rows, :], w2[...], 1, 0) + b2[...]
        if keep is not None:
            keep[3][rows, :] = mixed
        give(half, x[half * HS : half * HS + HS].reshape(HR, D) + ls[...] * mixed)


def unpadded(values):
    col = lax.broadcasted_iota(jnp.int32, values.shape, 1)
    return jnp.where(col < S, values, 0.0)


def to_section(src, dst, send, recv, section):
    return pltpu.make_async_remote_copy(
        src_ref=src,
        dst_ref=dst,
        send_sem=send,
        recv_sem=recv,
        device_id={"section": section},
        device_id_type=MESH,
    )


def greet_sections(barrier):
    s = lax.axis_index("section")
    count = lax.axis_size("section")
    for other in (lax.rem(s + 1, count), lax.rem(s + count - 1, count)):
        pl.semaphore_signal(barrier, inc=1, device_id={"section": other}, device_id_type=MESH)


def train_kernel(
    sources, marked,
    inputs, cot, probe, k, kb, gain, nb, w1, b1, w2, b2, ls,
    o_w1, o_w2, o_probe,
    w1f, w2f, w1b, w2b, x, sh, shd, conv, xhat, rstd, nrm, h, gp, mixed, dmb, du, dc, g,
    pt, gkb, ggain, gnb, gb1, gb2, gls, tiles, outgoing, incoming,
    fsend, frecv, bsend, brecv, f_s, f_r, b_s, b_r, w_in, w_out, e_s, e_r, block_of, relay, r_s, r_r,
    o_k, o_kb, o_gain, o_nb, o_b1, o_b2, o_ls,
):
    s = lax.axis_index("section")
    last = lax.axis_size("section") - 1
    up = jnp.minimum(s + 1, last)
    down = jnp.maximum(s - 1, 0)
    me = lax.axis_index("member")

    loads = [
        pltpu.make_async_copy(w1, w1f, w_in.at[0]),
        pltpu.make_async_copy(w2, w2f, w_in.at[1]),
    ]
    for load in loads:
        load.start()
    barrier = pltpu.get_barrier_semaphore()
    greet_sections(barrier)
    for t in ORDER:
        pl.semaphore_signal(
            barrier, inc=1, device_id={"member": at_distance(me, t)}, device_id_type=MESH
        )
    for ref in (pt, gkb, ggain, gnb, gb1, gb2, gls):
        ref[...] = jnp.zeros_like(ref)

    def tables():
        def per_slot(t):
            to = at_distance(me, t)
            block = jnp.int32(0)
            for b in range(32):
                block = jnp.where((sources[b, to] == me) & (marked[b] == 1), b, block)
            block_of[t] = block

        loop(32, per_slot)

    @pl.when(s > 0)
    def _():
        tables()

    def take(half, first, given, arrived, wait, dst):
        rows = slice(half * HS, half * HS + HS)

        @pl.when(first)
        def _():
            dst[rows, S:W, :] = jnp.zeros((HS, W - S, D), F32)
            dst[rows, 0:S, :] = given[rows].astype(F32)

        @pl.when(jnp.logical_not(first))
        def _():
            wait()
            dst[rows] = arrived[rows].astype(F32)

    def half_copy(send, recv, sems, j, half, section):
        rows = pl.ds(half * HS, HS)
        return to_section(
            send.at[j, rows], recv.at[j, rows], sems[0].at[j, half], sems[1].at[j, half], section
        )

    def fwd_copy(j, half):
        return half_copy(fsend, frecv, (f_s, f_r), j, half, up)

    pieces = ((0, HS - 3), (HS - 3, HS), (HS, S))

    def bwd_copy(j, piece):
        rows = pl.ds(pieces[piece][0], pieces[piece][1] - pieces[piece][0])
        return to_section(
            bsend.at[j, rows], brecv.at[j, rows], b_s.at[j, piece], b_r.at[j, piece], down
        )

    def fwd(j):
        rows = pl.ds(pl.multiple_of(j * R, R), R)

        def before():
            @pl.when(j == 0)
            def _():
                pl.semaphore_wait(barrier, 2 + len(ORDER))
                for load in loads:
                    load.wait()

                def cast(i):
                    r = pl.ds(pl.multiple_of(i * 32, 32), 32)
                    w1b[r, :] = w1f[r, :].astype(BF)
                    r = pl.ds(pl.multiple_of(i * 128, 128), 128)
                    w2b[r, :] = w2f[r, :].astype(BF)

                loop(16, cast)

        def give(half, values):
            @pl.when(s < last)
            def _():
                fsend[j, half * HS : half * HS + HS] = unpadded(values.reshape(HS, W, D)).astype(BF)
                fwd_copy(j, half).start()

        convolve(
            lambda half: take(
                half, s == 0, inputs.at[j], frecv.at[j], fwd_copy(j, half).wait_recv, x.at[j]
            ),
            x.at[j], sh.at[j], conv, k, kb,
        )
        before()
        mix(
            x.at[j], conv, gain, nb, w1b, b1, w2b, b2, ls, h.at[rows, :], nrm.at[rows, :], give,
            (xhat.at[j], rstd.at[j], gp.at[j], mixed.at[j]),
        )

    loop(2, fwd)

    @pl.when(s == 0)
    def _():
        tables()

    def kernel_grad(j):
        def per_lanes(c):
            lanes = lanes_of(c)
            for dj in range(7):
                acc = [None] * 7
                for r in range(S):
                    d = dc[j, r, :, lanes]
                    for di in range(7):
                        if 0 <= r + di - 3 < S:
                            p = d * sh[j, dj, r + di - 3, :, lanes]
                            acc[di] = p if acc[di] is None else acc[di] + p
                for di in range(7):
                    pt[di, dj, :, lanes] += acc[di][0:8] + acc[di][8:16]

        loop(D // LANE, per_lanes)

    def bwd(j):
        def send_back(piece):
            part = slice(*pieces[piece])
            bsend[j, part] = unpadded(g[part] + conv[part]).astype(BF)
            bwd_copy(j, piece).start()

        def nothing(r, lanes):
            return jnp.zeros((W, LANE), F32)

        for half in range(2):
            base = pl.multiple_of(j * R, R)
            rows = slice(half * HR, half * HR + HR)
            both = half_rows(half, base)

            def arrive(half=half):
                for piece in ((0, 1), (2,))[half]:
                    bwd_copy(j, piece).wait_recv()

            take(half, s == last, cot.at[j], brecv.at[j], arrive, g)
            flat = g[half * HS : half * HS + HS].reshape(HR, D)
            dm = flat * ls[...]
            dmb[both, :] = dm.astype(BF)
            gb2[...] += jnp.sum(dm, axis=0, keepdims=True)
            gls[...] += jnp.sum(flat * mixed[j, rows, :], axis=0, keepdims=True)
            for c in range(HID // CH):
                cols = slice(c * CH, c * CH + CH)
                a = dot(dmb[both, :], w2b[cols, :], 1, 1) * gp[j, rows, cols]
                du[both, cols] = a.astype(BF)
                gb1[:, cols] += jnp.sum(a, axis=0, keepdims=True)
            dn = dot(du[both, :], w1b[...], 1, 1)
            hat = xhat[j, rows, :]
            dh = dn * gain[...]
            m1 = jnp.mean(dh, axis=-1, keepdims=True)
            m2 = jnp.mean(dh * hat, axis=-1, keepdims=True)
            d = rstd[j, rows, :] * (dh - m1 - hat * m2)
            dc[j, half * HS : half * HS + HS] = d.reshape(HS, W, D)
            ggain[...] += jnp.sum(dn * hat, axis=0, keepdims=True)
            gnb[...] += jnp.sum(dn, axis=0, keepdims=True)
            gkb[...] += jnp.sum(d, axis=0, keepdims=True)

            @pl.when(s > 0)
            def _(half=half):
                conv_half(dc.at[j], shd, k, conv, nothing, half, True)
                for piece in ((0,), (1, 2))[half]:
                    send_back(piece)

    loop(2, bwd)

    for c in range(4):
        cols = pl.ds(c * 512, 512)
        new = w1f[:, cols] - learning_rate * dot(nrm[...], du[:, cols], 0, 0)
        w1f[:, cols] = new
        for q in range(4):
            tiles[4 * c + q] = new[:, q * TILE : (q + 1) * TILE].astype(BF)
    for r in range(HID // D):
        rows = pl.ds(r * D, D)
        new = w2f[rows, :] - learning_rate * dot(h[:, rows], dmb[...], 0, 0)
        w2f[rows, :] = new
        for q in range(4):
            tiles[16 + 4 * q + r] = new[:, q * TILE : (q + 1) * TILE].astype(BF)

    def push_copy(t):
        return pltpu.make_async_remote_copy(
            src_ref=outgoing.at[t],
            dst_ref=incoming.at[t],
            send_sem=e_s.at[t],
            recv_sem=e_r.at[t],
            device_id={"member": at_distance(me, t)},
            device_id_type=MESH,
        )

    partner = last - s

    def is_relayed(i):
        return s < (2 if i < BOTH else 1)

    def is_relay(i):
        return partner < (2 if i < BOTH else 1)

    def relay_copy(i):
        return to_section(
            outgoing.at[RELAYED[i]], relay.at[0, i], e_s.at[RELAYED[i]], r_r.at[0, i], partner
        )

    def relay_across(i):
        return pltpu.make_async_remote_copy(
            src_ref=relay.at[0, i],
            dst_ref=relay.at[1, i],
            send_sem=r_s.at[0, i],
            recv_sem=r_r.at[1, i],
            device_id={"member": at_distance(me, RELAYED[i])},
            device_id_type=MESH,
        )

    def relay_back(i):
        return to_section(
            relay.at[1, i], incoming.at[RELAYED[i]], r_s.at[1, i], e_r.at[RELAYED[i]], partner
        )

    def push(t):
        outgoing[t] = tiles[block_of[t]]
        if t in RELAYED:

            i = RELAYED.index(t)

            @pl.when(is_relayed(i))
            def _():
                relay_copy(i).start()

            @pl.when(jnp.logical_not(is_relayed(i)))
            def _():
                push_copy(t).start()
        else:
            push_copy(t).start()

    for t in SEQUENCE[:EARLY]:
        push(t)

    later = list(SEQUENCE[EARLY:])
    for i in range(len(RELAYED) + 1):
        if i < len(RELAYED):

            @pl.when(is_relay(i))
            def _(i=i):
                relay_copy(i).wait_recv()
                relay_across(i).start()

        if i > 0:

            @pl.when(is_relay(i - 1))
            def _(i=i - 1):
                relay_across(i).wait_recv()
                relay_back(i).start()

        push(later.pop(0))
    for t in later:
        push(t)

    loop(2, kernel_grad)
    for di in range(7):
        for dj in range(7):
            o_k[di, dj] = k[di, dj] - learning_rate * jnp.sum(pt[di, dj], axis=0, keepdims=True)
    for old, grad, new in (
        (kb, gkb, o_kb), (gain, ggain, o_gain), (nb, gnb, o_nb),
        (b1, gb1, o_b1), (b2, gb2, o_b2), (ls, gls, o_ls),
    ):
        new[...] = old[...] - learning_rate * grad[...]

    def probe_take(half):
        take(half, s == 0, probe, frecv.at[2], fwd_copy(2, half).wait_recv, x.at[0])

    def probe_give(half, values):
        rows = slice(half * HS, half * HS + HS)
        fsend[2, rows] = unpadded(values.reshape(HS, W, D)).astype(BF)

        @pl.when(s < last)
        def _():
            fwd_copy(2, half).start()

        o_probe[rows] = fsend[2, rows, 0:S, :]

    @pl.when(s == 0)
    def _():
        convolve(probe_take, x.at[0], shd, conv, o_k, o_kb)

    for t in ORDER:
        push_copy(t).wait_recv()

    def slot_of(b):
        source = sources[b, me]
        z = lax.rem(me // 8 - source // 8 + 4, 4)
        x = lax.rem(lax.rem(me // 2, 4) - lax.rem(source // 2, 4) + 4, 4)
        c = lax.rem(lax.rem(me, 2) + lax.rem(source, 2), 2)
        return z * 8 + x * 2 + c

    def place_in(b):
        w1b[:, lanes_of(b)] = jnp.where(marked[b] == 1, incoming[slot_of(b)], tiles[b])

    loop(16, place_in)

    def place_out(r):
        for c in range(4):
            b = 16 + 4 * c + r
            w2b[pl.ds(pl.multiple_of(r * D, D), D), pl.ds(c * TILE, TILE)] = jnp.where(
                marked[b] == 1, incoming[slot_of(b)], tiles[b]
            )

    loop(4, place_out)

    stores = [
        pltpu.make_async_copy(w1f, o_w1, w_out.at[0]),
        pltpu.make_async_copy(w2f, o_w2, w_out.at[1]),
    ]

    def finish():
        def finish_in(b):
            lanes = lanes_of(b)
            w1f[:, lanes] = jnp.where(marked[b] == 1, w1b[:, lanes].astype(F32), w1f[:, lanes])

        def finish_out(r):
            rows = pl.ds(pl.multiple_of(r * D, D), D)
            for c in range(4):
                cols = pl.ds(c * TILE, TILE)
                w2f[rows, cols] = jnp.where(
                    marked[16 + 4 * c + r] == 1, w2b[rows, cols].astype(F32), w2f[rows, cols]
                )

        loop(16, finish_in)
        stores[0].start()
        loop(4, finish_out)
        stores[1].start()

    @pl.when(s > 0)
    def _():
        finish()
        convolve(probe_take, x.at[0], shd, conv, o_k, o_kb)

    mix(
        x.at[0], conv, o_gain, o_nb, w1b, o_b1, w2b, o_b2, o_ls,
        h.at[pl.ds(0, R), :], nrm.at[pl.ds(0, R), :], probe_give, None,
    )

    @pl.when(s == 0)
    def _():
        finish()

    for copy in stores:
        copy.wait()
    for t in ORDER:
        push_copy(t).wait_send()

    for i in range(len(RELAYED)):

        @pl.when(is_relay(i))
        def _(i=i):
            relay_across(i).wait_send()
            relay_back(i).wait_send()

    for half in range(2):
        for j in range(3):

            @pl.when(s < last)
            def _(j=j, half=half):
                fwd_copy(j, half).wait_send()

    for piece in range(3):
        for j in range(2):

            @pl.when(s > 0)
            def _(j=j, piece=piece):
                bwd_copy(j, piece).wait_send()


def vmem(n):
    return [pl.BlockSpec(memory_space=pltpu.VMEM)] * n


def hbm(n):
    return [pl.BlockSpec(memory_space=pltpu.HBM)] * n


def params(collective, mib):
    return pltpu.CompilerParams(
        collective_id=collective, has_side_effects=True, vmem_limit_bytes=mib * 2**20
    )


def train(tables, inputs, cot, probe, small, w1, w2):
    k, kb, gain, nb, b1, b2, ls = small
    dma = pltpu.SemaphoreType.DMA
    V = pltpu.VMEM
    shape = jax.ShapeDtypeStruct
    wide = (2, S, W, D)
    return pl.pallas_call(
        train_kernel,
        out_shape=(shape((D, HID), F32), shape((HID, D), F32), shape((S, S, D), BF)),
        in_specs=[pl.BlockSpec(memory_space=pltpu.SMEM)] * 2 + vmem(7) + hbm(1) + vmem(1) + hbm(1) + vmem(2),
        out_specs=hbm(2) + vmem(1),
        scratch_shapes=[
            V((D, HID), F32), V((HID, D), F32), V((D, HID), BF), V((HID, D), BF),
            V(wide, F32), V((2, 7, S, W, D), F32), V((7, S, W, D), F32), V((S, W, D), F32),
            V((2, R, D), F32), V((2, R, 1), F32), V((2 * R, D), BF), V((2 * R, HID), BF),
            V((2, R, HID), F32), V((2, R, D), F32), V((2 * R, D), BF), V((2 * R, HID), BF),
            V(wide, F32), V((S, W, D), F32),
            V((7, 7, 8, D), F32), V((1, D), F32), V((1, D), F32), V((1, D), F32),
            V((1, HID), F32), V((1, D), F32), V((1, D), F32),
            V((32, D, TILE), BF), V((32, D, TILE), BF), V((32, D, TILE), BF),
            V((3, S, W, D), BF), V((3, S, W, D), BF), V(wide, BF), V(wide, BF),
            dma((3, 2)), dma((3, 2)), dma((2, 3)), dma((2, 3)), dma((2,)), dma((2,)),
            dma((32,)), dma((32,)), pltpu.SMEM((32,), jnp.int32),
            V((2, len(RELAYED), D, TILE), BF), dma((2, len(RELAYED))), dma((2, len(RELAYED))),
            V((7, 7, 1, D), F32), V((1, D), F32), V((1, D), F32), V((1, D), F32),
            V((1, HID), F32), V((1, D), F32), V((1, D), F32),
        ],
        compiler_params=params(0, 60),
        name="train",
    )(*tables, inputs, cot, probe, k, kb, gain, nb, w1, b1, w2, b2, ls)


def local(
    inputs, cotangent, probe, dw_kernel, dw_bias, norm_gain, norm_bias, w_in, b_in, w_out, b_out,
    layer_scale, shuffle_mask, source_member,
):
    small = (
        dw_kernel[0, 0][:, :, None, :], dw_bias[0], norm_gain[0], norm_bias[0], b_in[0], b_out[0],
        layer_scale[0],
    )
    marked = shuffle_mask[0]
    new_in, new_out, out = train(
        (source_member[0], marked), inputs[0, :, 0], cotangent[0, :, 0], probe[0, 0], small,
        w_in[0, 0], w_out[0, 0],
    )
    return new_in[None, None], new_out[None, None], out[None, None, None]


def solution(mesh):
    return jax.shard_map(
        local,
        mesh=mesh,
        in_specs=(
            P("member", None, None, None, None, None),
            P("member", None, None, None, None, None),
            P("member", None, None, None, None),
            P("member", "section", None, None, None),
            P("member", "section", None),
            P("member", "section", None),
            P("member", "section", None),
            P("member", "section", None, None),
            P("member", "section", None),
            P("member", "section", None, None),
            P("member", "section", None),
            P("member", "section", None),
            P("section", None),
            P("section", None, None),
        ),
        out_specs=(
            P("member", "section", None, None),
            P("member", "section", None, None),
            P("member", "section", None, None, None, None),
        ),
        check_vma=False,
    )
```
